32 devices in a mesh: groups: 2 (over y), ctx: 4 (over z), head: 4 (over x, core).
Axes of the slice: x: 2, y: 2, z: 4, core: 2. Of those that a mesh axis runs over, the one named last changes fastest.
Arguments:
- q_nope: bfloat16 [1024, 12288], P(('groups', 'ctx'), 'head'), parts along dimension 0, may hold values from -6 to 6
- q_rope: bfloat16 [1024, 6144], P(('groups', 'ctx'), 'head'), parts along dimension 0, may hold values from -56 to 56
- w_uk: bfloat16 [96, 128, 512], P('head'), may hold values from -0.5 to 0.5
- w_uv: bfloat16 [96, 512, 128], P('head'), may hold values from -0.25 to 0.25
- cache_latent: bfloat16 [256, 64, 512], P(('groups', 'ctx')), parts along dimension 0, may hold values from -6 to 6
- cache_rope: bfloat16 [256, 4096], P(('groups', 'ctx')), parts along dimension 0, may hold values from -6 to 6
- block_owner: int32 [256], P('groups'), parts along dimension 0, may hold values from 0 to 3, as said below
- selection: int32 [64, 32], P(('groups', 'ctx')), parts along dimension 0, may hold values from 0 to 127, as said below
Outputs:
- attn_out: bfloat16 [1024, 12288], P(('groups', 'ctx'), 'head'), parts along dimension 0
The draws below stay inside these ranges and needn't reach their ends.
There are 2 independent parts, one for each index of `groups`. The reference program is written for one: setup_inputs(seed, part) draws one part's arguments, and reference() takes and returns one part's arrays. A program takes and returns all parts, laid end to end along the dimension named above; an argument that names none is the same for every part. Nothing has to cross between parts.
Inputs may be any that keep to these rules, and one draw needn't show every extreme that they name: `selection`: row g serves queries g * 16 to g * 16 + 15 and names 32 different blocks: first the block that holds those queries, then the block before it, then blocks below (29) * 4. Over the 8 rows of one ctx index, at most 17 different blocks lie on any one owner, and on one owner, the same for every ctx index, exactly 17. `block_owner`: blocks k * 4 to k * 4 + 3 lie on 4 different owners; block b is row b // 4 of its owner's 32 rows.
All inputs are finite; a program needn't handle non-finite values.
Results may differ from the reference program's by a relative error of at most 0.0085.
Values may be sent and summed in bfloat16 or wider, within the bound.
A program may use at most 128 MiB of HBM per device.

```python
import jax
import jax.numpy as jnp
from jax import lax

DL = 512
DR = 64
DN = 128
DV = 128
HEADS = 96
BLK = 64
TOPB = 32
QG = 16
OWNERS = 4
QBLK = 2
NG = 8
BLK_DEV = 32
NBLK = 128
Q = 512
NGROUPS = 32
CONTEXT = 8192
CAP = 17


def owner_layout(key):
    key = jax.random.fold_in(key, 11)
    streams = jax.random.split(key, BLK_DEV)
    layout = jax.vmap(lambda stream: jax.random.permutation(stream, OWNERS))(streams)
    return layout.astype(jnp.int32)


def draw_block_owner(key, part):
    layout = owner_layout(key)
    return layout.reshape(-1)


def draw_selection(key, part):
    layout = owner_layout(key)
    key = jax.random.fold_in(key, 2)
    key_full, key_short, key_order, key_fill = jax.random.split(key, 4)
    owner_of = layout.reshape(-1)
    inverse = jnp.argsort(layout, axis=1).astype(jnp.int32)
    devices = jnp.arange(OWNERS, dtype=jnp.int32)
    first_span = NBLK - OWNERS * QBLK
    recent = first_span - 1 + devices[:, None] * QBLK + jnp.arange(QBLK + 1, dtype=jnp.int32)[None, :]
    recent_owner = owner_of[recent]
    own_count = jnp.sum((recent_owner[:, :, None] == devices[None, None, :]).astype(jnp.int32), axis=1)
    full_owner = jax.random.randint(key_full, (), 0, OWNERS)
    headroom = CAP - own_count
    shortfall = jax.random.randint(key_short, (OWNERS, OWNERS), 0, headroom // 2 + 1)
    taken = jnp.where(devices[None, :] == full_owner, headroom, headroom - shortfall)
    prior_groups = BLK_DEV - QBLK - 1
    shuffle = jax.random.randint(key_order, (OWNERS, OWNERS, prior_groups), 0, 1 << 20)
    ordering = jnp.argsort(shuffle * prior_groups + jnp.arange(prior_groups, dtype=jnp.int32), axis=2)[:, :, :CAP]
    ordering = ordering.astype(jnp.int32)
    owner_grid = jnp.broadcast_to(devices[None, :, None], ordering.shape)
    blocks = ordering * OWNERS + inverse[ordering, owner_grid]
    usable = jnp.arange(CAP, dtype=jnp.int32)[None, None, :] < taken[:, :, None]
    pool_width = OWNERS * CAP
    blocks = blocks.reshape(OWNERS, pool_width)
    usable = usable.reshape(OWNERS, pool_width)
    slot_ids = jnp.arange(pool_width, dtype=jnp.int32)
    packed = jnp.argsort(jnp.where(usable, slot_ids[None, :], pool_width + slot_ids[None, :]), axis=1)
    pool_blocks = jnp.take_along_axis(blocks, packed, axis=1)
    pool_size = jnp.sum(usable.astype(jnp.int32), axis=1)
    group_ids = jnp.arange(NG, dtype=jnp.int32)
    jitter = jax.random.randint(key_fill, (OWNERS, NG, pool_width), 0, 1 << 16)
    slot_grid = slot_ids[None, None, :]
    rank_key = jnp.where(slot_grid % NG == group_ids[None, :, None], slot_grid, pool_width + jitter * pool_width + slot_grid)
    rank_key = jnp.where(slot_grid < pool_size[:, None, None], rank_key, (1 << 28) + slot_grid)
    picked = jnp.argsort(rank_key, axis=2)[:, :, :TOPB - 2]
    spread = jnp.broadcast_to(pool_blocks[:, None, :], (OWNERS, NG, pool_width))
    chosen = jnp.take_along_axis(spread, picked, axis=2)
    own_block = first_span + devices[:, None] * QBLK + group_ids[None, :] // (BLK // QG)
    lists = jnp.concatenate([own_block[:, :, None], own_block[:, :, None] - 1, chosen], axis=2)
    return lists.reshape(NGROUPS, TOPB).astype(jnp.int32)


def draw_cache_rope(key, part):
    key = jax.random.fold_in(key, 21)
    values = jnp.clip(jax.random.normal(key, (NBLK, BLK * DR), jnp.float32), -6.0, 6.0)
    return values.astype(jnp.bfloat16)


def draw_q_rope(key, part):
    key = jax.random.fold_in(key, 22)
    values = jnp.clip(jax.random.normal(key, (Q, HEADS * DR), jnp.float32), -6.0, 6.0)
    return values.astype(jnp.bfloat16)


def block_scale(rng, extent, cuts, least, top_value):
    factor_of = 1.0
    for axis_at, parts in cuts:
        draws = jax.random.uniform(jax.random.fold_in(jax.random.fold_in(rng, 6), axis_at), (parts,), jnp.float32, least / len(cuts), top_value / len(cuts))
        factor_of = factor_of * jnp.repeat(jnp.exp(draws), extent[axis_at] // parts).reshape((-1,) + (1,) * (len(extent) - 1 - axis_at))
    return factor_of


def gaussian(stream_key, shape, deviation, limit, cuts=(), kind=jnp.bfloat16):
    drawn = deviation * jax.random.normal(stream_key, shape, jnp.float32)
    if cuts:
        drawn = drawn * block_scale(stream_key, shape, cuts, -0.22, 0.18)
    return jnp.clip(drawn, -limit, limit).astype(kind)


def setup_inputs(seed: int = 0, part: int = 0) -> dict:
    key_list = jax.random.split(jax.random.key(seed), 9)
    part_keys = jax.random.split(jax.random.fold_in(key_list[8], part), 9)
    return {
        "q_nope": gaussian(part_keys[0], (Q, HEADS * DN), 1.0, 6.0, ((0, 4), (1, 4))),
        "q_rope": draw_q_rope(jax.random.fold_in(jax.random.fold_in(key_list[8], part), 71), part),
        "w_uk": gaussian(key_list[2], (HEADS, DN, DL), DN ** -0.5, 0.5, ((0, 4),)),
        "w_uv": gaussian(key_list[3], (HEADS, DL, DV), DL ** -0.5, 0.25, ((0, 4),)),
        "cache_latent": gaussian(part_keys[4], (NBLK, BLK, DL), 1.0, 6.0, ((0, 4),)),
        "cache_rope": draw_cache_rope(jax.random.fold_in(jax.random.fold_in(key_list[8], part), 71), part),
        "block_owner": draw_block_owner(jax.random.fold_in(jax.random.fold_in(key_list[8], part), 71), part),
        "selection": draw_selection(jax.random.fold_in(jax.random.fold_in(key_list[8], part), 71), part),
    }


def reference(q_nope, q_rope, w_uk, w_uv, cache_latent, cache_rope, block_owner, selection):
    block_ids = jnp.arange(NBLK, dtype=jnp.int32)
    row_of = (block_owner * BLK_DEV + block_ids // OWNERS).astype(jnp.int32)
    uk_float = w_uk.astype(jnp.float32)
    uv_float = w_uv.astype(jnp.float32)
    softmax_scale = (DN + DR) ** -0.5
    token_ids = jnp.arange(BLK, dtype=jnp.int32)

    def one_group(group_id):
        picked = selection[group_id]
        cache_rows = row_of[picked]
        key_latent = cache_latent[cache_rows].reshape(TOPB * BLK, DL).astype(jnp.float32)
        key_rope = cache_rope[cache_rows].reshape(TOPB * BLK, DR).astype(jnp.float32)
        first_row = (group_id * QG).astype(jnp.int32)
        query_nope = lax.dynamic_slice_in_dim(q_nope, first_row, QG, 0).reshape(QG, HEADS, DN).astype(jnp.float32)
        query_rope = lax.dynamic_slice_in_dim(q_rope, first_row, QG, 0).reshape(QG, HEADS, DR).astype(jnp.float32)
        query_latent = jnp.einsum("qhd,hdc->qhc", query_nope, uk_float).astype(jnp.bfloat16)
        query_latent = lax.optimization_barrier(query_latent).astype(jnp.float32)
        scores = jnp.einsum("qhc,kc->qhk", query_latent, key_latent) + jnp.einsum("qhr,kr->qhk", query_rope, key_rope)
        scores = scores * softmax_scale
        query_pos = CONTEXT - Q + first_row + jnp.arange(QG, dtype=jnp.int32)
        key_pos = (picked[:, None] * BLK + token_ids[None, :]).reshape(-1)
        allowed = key_pos[None, None, :] <= query_pos[:, None, None]
        scores = jnp.where(allowed, scores, -jnp.inf)
        row_max = jnp.max(scores, axis=-1, keepdims=True)
        shifted = jnp.exp(scores - row_max)
        weights = (shifted / jnp.sum(shifted, axis=-1, keepdims=True)).astype(jnp.bfloat16)
        weights = lax.optimization_barrier(weights).astype(jnp.float32)
        out_latent = jnp.einsum("qhk,kc->qhc", weights, key_latent).astype(jnp.bfloat16)
        out_latent = lax.optimization_barrier(out_latent).astype(jnp.float32)
        result = jnp.einsum("qhc,hcv->qhv", out_latent, uv_float).astype(jnp.bfloat16)
        return result.reshape(QG, HEADS * DV)

    stacked = lax.map(one_group, jnp.arange(NGROUPS, dtype=jnp.int32))
    return stacked.reshape(Q, HEADS * DV)
```

```python
import functools
import math

import jax
import jax.numpy as jnp
from jax import lax
from jax.experimental import pallas as pl
from jax.experimental.pallas import tpu as pltpu
from jax.sharding import PartitionSpec as P

LANES = 128
PIECES = 4
VMEM_BYTES = 56 * 1024 * 1024
MESH = pl.DeviceIdType.MESH


def slot_lists(present, owned, capacity, owners):
    member = present * owned
    ranking = jnp.cumsum(member) - 1
    local_row = lax.broadcasted_iota(jnp.int32, present.shape, 0) // owners
    slot_ids = lax.broadcasted_iota(jnp.int32, (capacity,) + present.shape, 0)
    matched = (ranking[None, :] == slot_ids) & (member[None, :] > 0)
    listing = jnp.sum(jnp.where(matched, local_row[None, :], 0), axis=1)
    return (listing, jnp.where(member > 0, ranking, 0))


def pack_blocks(latent_rows, rope_rows):
    rows, block_len, latent = latent_rows.shape
    lat = latent_rows.reshape(rows, block_len, latent // LANES, LANES)
    lat = lat.transpose(0, 2, 1, 3).reshape(rows, -1, LANES)
    return jnp.concatenate([lat, rope_rows], axis=1)


def split_rope(cache_rope, block_len):
    rows = cache_rope.shape[0]
    halves = cache_rope.reshape(rows, 2, block_len // 2, -1)
    return halves.transpose(0, 2, 1, 3).reshape(rows, block_len // 2, -1)


def project_queries(nope_ref, rope_ref, uk_ref, qfull_ref):
    head_count, head_dim, latent = uk_ref.shape
    groups = qfull_ref.shape[0]
    size = qfull_ref.shape[1] // head_count
    half = LANES // 2

    def one_pair(pair, carry):
        slab = rope_ref[:, pl.ds(pl.multiple_of(pair * LANES, LANES), LANES)].astype(jnp.float32)
        turned = pltpu.roll(slab, half, 1)
        low = lax.broadcasted_iota(jnp.int32, slab.shape, 1) < half
        twice = (jnp.where(low, slab, turned), jnp.where(low, turned, slab))
        for odd in range(2):
            head = pair * 2 + odd
            query = nope_ref[:, pl.ds(pl.multiple_of(head * head_dim, LANES), head_dim)]
            lat = jnp.dot(query, uk_ref[head], preferred_element_type=jnp.float32)
            lat = lat.astype(jnp.bfloat16).reshape(groups, size, latent)
            rot = twice[odd].astype(jnp.bfloat16).reshape(groups, size, LANES)
            at = pl.ds(pl.multiple_of(head * size, size), size)
            qfull_ref[:, at, :latent] = lat
            qfull_ref[:, at, latent:] = rot
        return carry

    lax.fori_loop(0, head_count // 2, one_pair, 0)


def query_kernel(nope_ref, rope_ref, uk_ref, qfull_ref):
    project_queries(nope_ref, rope_ref, uk_ref, qfull_ref)


def gather_kernel(
    ctx_size, head_size, nope_ref, rope_ref, uk_ref, lat_ref, krope_ref, all_ref, qfull_ref,
    packed, local_sem, right_send, right_recv, left_send, left_recv, x_send, x_recv, z_core_send, z_core_recv,
    x_core_send, x_core_recv,
):
    ctx = lax.axis_index("ctx")
    head = lax.axis_index("head")
    across = (head + head_size // 2) % head_size
    sibling = head + 1 - 2 * (head % 2)
    rows = lat_ref.shape[0]
    quarter = rows // head_size
    piece = quarter // PIECES
    block_len = lat_ref.shape[1]
    lane_groups = lat_ref.shape[2] // LANES
    has_left = ctx > 0
    has_right = ctx < ctx_size - 1

    barrier = pltpu.get_barrier_semaphore()
    pl.semaphore_signal(barrier, inc=1, device_id={"head": across}, device_id_type=MESH)
    pl.semaphore_signal(barrier, inc=1, device_id={"head": sibling}, device_id_type=MESH)

    @pl.when(has_left)
    def _():
        pl.semaphore_signal(barrier, inc=1, device_id={"ctx": ctx - 1}, device_id_type=MESH)

    @pl.when(has_right)
    def _():
        pl.semaphore_signal(barrier, inc=1, device_id={"ctx": ctx + 1}, device_id_type=MESH)

    def pack_row(row, carry):
        for group in range(lane_groups):
            packed[row, group * block_len:(group + 1) * block_len, :] = lat_ref[
                row, :, group * LANES:(group + 1) * LANES
            ]
        packed[row, lane_groups * block_len:, :] = krope_ref[row]
        return carry

    lax.fori_loop(0, rows, pack_row, 0)
    pl.semaphore_wait(barrier, 2 + has_left.astype(jnp.int32) + has_right.astype(jnp.int32))

    own = pltpu.make_async_copy(packed, all_ref.at[pl.ds(ctx * rows, rows)], local_sem)
    own.start()

    def place(shard, part, k):
        return all_ref.at[pl.ds(shard * rows + part * quarter + k * piece, piece)]

    def hop(source, target, send, recv, device):
        return pltpu.make_async_remote_copy(
            src_ref=source, dst_ref=target, send_sem=send, recv_sem=recv, device_id=device, device_id_type=MESH
        )

    def send_right(source, shard, k, at):
        return hop(source, place(shard, head, k), right_send.at[at], right_recv.at[at], {"ctx": ctx + 1})

    def send_left(source, shard, k, at):
        return hop(source, place(shard, head, k), left_send.at[at], left_recv.at[at], {"ctx": ctx - 1})

    def start_own(k, carry):
        source = packed.at[pl.ds(head * quarter + k * piece, piece)]

        @pl.when(has_right)
        def _():
            send_right(source, ctx, k, k).start()

        @pl.when(has_left)
        def _():
            send_left(source, ctx, k, k).start()

        return carry

    lax.fori_loop(0, PIECES, start_own, 0)
    project_queries(nope_ref, rope_ref, uk_ref, qfull_ref)

    events = (ctx_size - 1) * PIECES

    def x_copy(side, at, shard, k, part):
        ref = place(shard, part, k)
        return hop(ref, ref, x_send.at[side, at], x_recv.at[side, at], {"head": across})

    def z_core_copy(side, at, shard, k, part):
        ref = place(shard, part, k)
        return hop(ref, ref, z_core_send.at[side, at], z_core_recv.at[side, at], {"head": sibling})

    def x_core_copy(side, at, shard, k, part):
        ref = place(shard, part, k)
        return hop(ref, ref, x_core_send.at[side, at], x_core_recv.at[side, at], {"head": sibling})

    def sides(at):
        step = at // PIECES
        return (
            (0, ctx - 1 - step, ctx - 1 - step >= 0),
            (1, ctx + 1 + step, ctx + 1 + step <= ctx_size - 1),
        )

    def from_z(at):
        k = at % PIECES
        for side, shard, there in sides(at):

            @pl.when(there)
            def _(side=side, shard=shard):
                if side == 0:
                    send_right(place(shard, head, k), shard, k, at).wait_recv()

                    @pl.when(has_right)
                    def _():
                        send_right(place(shard, head, k), shard, k, at + PIECES).start()
                else:
                    send_left(place(shard, head, k), shard, k, at).wait_recv()

                    @pl.when(has_left)
                    def _():
                        send_left(place(shard, head, k), shard, k, at + PIECES).start()

                x_copy(side, at, shard, k, head).start()
                z_core_copy(side, at, shard, k, head).start()

    def from_x(at):
        k = at % PIECES
        for side, shard, there in sides(at):

            @pl.when(there)
            def _(side=side, shard=shard):
                x_copy(side, at, shard, k, across).wait_recv()
                x_core_copy(side, at, shard, k, across).start()

    def event(at, carry):
        @pl.when(at < events)
        def _():
            from_z(at)

        @pl.when(at > 0)
        def _():
            from_x(at - 1)

        return carry

    lax.fori_loop(0, events + 1, event, 0)
    own.wait()

    def finish(at, carry):
        k = at % PIECES
        sibling_across = (sibling + head_size // 2) % head_size
        for side, shard, there in sides(at):

            @pl.when(there)
            def _(side=side, shard=shard):
                z_core_copy(side, at, shard, k, sibling).wait_recv()
                x_core_copy(side, at, shard, k, sibling_across).wait_recv()
                x_copy(side, at, shard, k, head).wait_send()
                z_core_copy(side, at, shard, k, head).wait_send()
                x_core_copy(side, at, shard, k, across).wait_send()
                if side == 0:

                    @pl.when(has_right)
                    def _():
                        send_right(place(shard, head, k), shard, k, at + PIECES).wait_send()
                else:

                    @pl.when(has_left)
                    def _():
                        send_left(place(shard, head, k), shard, k, at + PIECES).wait_send()

        return carry

    lax.fori_loop(0, events, finish, 0)

    def finish_own(k, carry):
        source = packed.at[pl.ds(head * quarter + k * piece, piece)]

        @pl.when(has_right)
        def _():
            send_right(source, ctx, k, k).wait_send()

        @pl.when(has_left)
        def _():
            send_left(source, ctx, k, k).wait_send()

        return carry

    lax.fori_loop(0, PIECES, finish_own, 0)


def attend(block_rows, limit, q_ref, keys_ref, scores_ref, scale, block_len, latent, chunk):
    lane_groups = latent // LANES
    size = q_ref.shape[0]
    half = block_len // 2
    low = lax.broadcasted_iota(jnp.int32, (half, LANES), 1) < LANES // 2

    def values_of(row):
        return [
            keys_ref[row, group * block_len:(group + 1) * block_len, :] for group in range(lane_groups)
        ]

    def keys_of(row):
        rope = keys_ref[row, lane_groups * block_len:, :]
        zero = jnp.zeros_like(rope)
        both = jnp.concatenate([jnp.where(low, rope, zero), jnp.where(low, zero, rope)], axis=0)
        return values_of(row) + [both]

    def stack(rows, parts_of):
        return jnp.concatenate([jnp.concatenate(parts_of(row), axis=1) for row in rows], axis=0)

    width = chunk * block_len
    count = len(block_rows) // chunk
    query = q_ref[...]
    top = None
    for c in range(count):
        keys = stack(block_rows[c * chunk:(c + 1) * chunk], keys_of)
        score = lax.dot_general(query, keys, (((1,), (1,)), ((), ())), preferred_element_type=jnp.float32)
        if c == 0:
            head_part = score[:, :LANES]
            lane = lax.broadcasted_iota(jnp.int32, head_part.shape, 1)
            barred = (lane < block_len) & (lane > limit)
            score = jnp.concatenate([jnp.where(barred, -jnp.inf, head_part), score[:, LANES:]], axis=1)
        scores_ref[:, c * width:(c + 1) * width] = score
        for at in range(width // LANES):
            part = score[:, at * LANES:(at + 1) * LANES]
            top = part if top is None else jnp.maximum(top, part)
    factor = scale * math.log2(math.e)
    shift = jnp.max(top, axis=1, keepdims=True) * factor
    total = jnp.zeros((size, LANES), jnp.float32)
    out = jnp.zeros((size, latent), jnp.float32)
    for c in range(count):
        weight = jnp.exp2(scores_ref[:, c * width:(c + 1) * width] * factor - shift)
        for at in range(width // LANES):
            total = total + weight[:, at * LANES:(at + 1) * LANES]
        values = stack(block_rows[c * chunk:(c + 1) * chunk], values_of)
        out = out + jnp.dot(weight.astype(jnp.bfloat16), values, preferred_element_type=jnp.float32)
    return out / jnp.sum(total, axis=1, keepdims=True)


def attention_kernel(
    scale, block_len, rows_ref, limit_ref, qfull_ref, keys_ref, uv_ref, out_ref, scores, out_latent
):
    head_count, latent, value_dim = uv_ref.shape
    groups = qfull_ref.shape[0]
    size = qfull_ref.shape[1] // head_count
    picks = rows_ref.shape[1]

    def one_list(g, carry):
        block_rows = [rows_ref[g, j] for j in range(picks)]
        query_at = lax.broadcasted_iota(jnp.int32, (qfull_ref.shape[1], LANES), 0) % size
        limit = limit_ref[g] + query_at
        found = attend(
            block_rows, limit, qfull_ref.at[g], keys_ref, scores, scale, block_len, latent, 4
        )
        out_latent[g] = found.astype(jnp.bfloat16)
        return carry

    lax.fori_loop(0, groups, one_list, 0)

    def one_head(h, carry):
        part = out_latent[:, pl.ds(pl.multiple_of(h * size, size), size), :].reshape(groups * size, latent)
        result = jnp.dot(part, uv_ref[h], preferred_element_type=jnp.float32)
        out_ref[:, pl.ds(pl.multiple_of(h * value_dim, LANES), value_dim)] = result.astype(jnp.bfloat16)
        return carry

    lax.fori_loop(0, head_count, one_head, 0)


def on_device(q_nope, q_rope, w_uk, w_uv, cache_latent, cache_rope, block_owner, selection):
    owners = lax.axis_size("ctx")
    heads = lax.axis_size("head")
    my_index = lax.axis_index("ctx")
    query_count = q_nope.shape[0]
    head_count, head_dim, latent = w_uk.shape
    value_dim = w_uv.shape[2]
    cache_rows, block_len = cache_latent.shape[:2]
    rope_dim = cache_rope.shape[1] // block_len
    group_count, pick_count = selection.shape
    block_count = block_owner.shape[0]
    query_blocks = query_count // block_len
    capacity = max(3 + query_blocks // 8, (2 * pick_count + 2 * query_blocks) // owners)
    group_size = query_count // group_count
    block_ids = lax.broadcasted_iota(jnp.int32, (block_count,), 0)
    rope_rows = split_rope(cache_rope, block_len)
    packed_rows = latent // LANES * block_len + block_len // 2
    qfull_shape = jax.ShapeDtypeStruct((group_count, head_count * group_size, latent + LANES), jnp.bfloat16)
    vmem = pl.BlockSpec(memory_space=pltpu.VMEM)
    smem = pl.BlockSpec(memory_space=pltpu.SMEM)

    if cache_rows <= 2 * capacity:
        position = block_owner * cache_rows + block_ids // owners
        events = (owners - 1) * PIECES
        pairs = [pltpu.SemaphoreType.DMA((events + PIECES,))] * 4 + [pltpu.SemaphoreType.DMA((2, events))] * 6
        keys, qfull = pl.pallas_call(
            functools.partial(gather_kernel, owners, heads),
            out_shape=(
                jax.ShapeDtypeStruct((owners * cache_rows, packed_rows, LANES), jnp.bfloat16),
                qfull_shape,
            ),
            in_specs=[vmem] * 5,
            out_specs=(pl.BlockSpec(memory_space=pl.ANY), vmem),
            scratch_shapes=[
                pltpu.VMEM((cache_rows, packed_rows, LANES), jnp.bfloat16),
                pltpu.SemaphoreType.DMA(()),
            ] + pairs,
            compiler_params=pltpu.CompilerParams(
                collective_id=0, has_side_effects=True, vmem_limit_bytes=VMEM_BYTES
            ),
        )(q_nope, q_rope, w_uk, cache_latent, rope_rows)
    else:
        owner_ids = lax.broadcasted_iota(jnp.int32, (owners, block_count), 0)
        owned_all = (block_owner[None, :] == owner_ids).astype(jnp.int32)
        present = jnp.zeros((block_count,), jnp.int32).at[selection.reshape(-1)].set(1)
        listings, ranking = jax.vmap(lambda owned: slot_lists(present, owned, capacity, owners))(
            owned_all
        )
        position = block_owner * capacity + jnp.sum(ranking, axis=0)
        wanted = lax.all_to_all(listings, "ctx", split_axis=0, concat_axis=0, tiled=True)
        flat_rows = wanted.reshape(-1)
        asked = pack_blocks(cache_latent[flat_rows], rope_rows[flat_rows])
        asked = asked.reshape(owners, capacity, packed_rows, LANES)
        keys = lax.all_to_all(asked, "ctx", split_axis=0, concat_axis=0, tiled=True)
        keys = keys.reshape(owners * capacity, packed_rows, LANES)
        qfull = pl.pallas_call(
            query_kernel,
            out_shape=qfull_shape,
            in_specs=[vmem] * 3,
            out_specs=vmem,
            compiler_params=pltpu.CompilerParams(vmem_limit_bytes=VMEM_BYTES),
        )(q_nope, q_rope, w_uk)

    first_pos = block_count * block_len - query_count * owners + my_index * query_count
    limits = first_pos + jnp.arange(group_count, dtype=jnp.int32) * group_size - selection[:, 0] * block_len
    return pl.pallas_call(
        functools.partial(attention_kernel, (head_dim + rope_dim) ** (-0.5), block_len),
        out_shape=jax.ShapeDtypeStruct((query_count, head_count * value_dim), jnp.bfloat16),
        in_specs=[smem, smem, vmem, vmem, vmem],
        out_specs=vmem,
        scratch_shapes=[
            pltpu.VMEM((head_count * group_size, pick_count * block_len), jnp.float32),
            pltpu.VMEM((group_count, head_count * group_size, latent), jnp.bfloat16),
        ],
        compiler_params=pltpu.CompilerParams(vmem_limit_bytes=VMEM_BYTES),
    )(position[selection], limits, qfull, keys, w_uv)


def solution(mesh):
    return jax.shard_map(
        on_device,
        mesh=mesh,
        in_specs=(
            P(("groups", "ctx"), "head"),
            P(("groups", "ctx"), "head"),
            P("head", None, None),
            P("head", None, None),
            P(("groups", "ctx"), None, None),
            P(("groups", "ctx"), None),
            P("groups"),
            P(("groups", "ctx"), None),
        ),
        out_specs=P(("groups", "ctx"), "head"),
        check_vma=False,
    )
```

```python
import functools
import math

import jax
import jax.numpy as jnp
from jax import lax
from jax.experimental import pallas as pl
from jax.experimental.pallas import tpu as pltpu
from jax.sharding import PartitionSpec as P

LANES = 128
PIECES = 4
VMEM_BYTES = 56 * 1024 * 1024
MESH = pl.DeviceIdType.MESH


def slot_lists(present, owned, capacity, owners):
    member = present * owned
    ranking = jnp.cumsum(member) - 1
    local_row = lax.broadcasted_iota(jnp.int32, present.shape, 0) // owners
    slot_ids = lax.broadcasted_iota(jnp.int32, (capacity,) + present.shape, 0)
    matched = (ranking[None, :] == slot_ids) & (member[None, :] > 0)
    listing = jnp.sum(jnp.where(matched, local_row[None, :], 0), axis=1)
    return (listing, jnp.where(member > 0, ranking, 0))


def pack_blocks(latent_rows, rope_rows):
    rows, block_len, latent = latent_rows.shape
    lat = latent_rows.reshape(rows, block_len, latent // LANES, LANES)
    lat = lat.transpose(0, 2, 1, 3).reshape(rows, -1, LANES)
    return jnp.concatenate([lat, rope_rows], axis=1)


def split_rope(cache_rope, block_len):
    rows = cache_rope.shape[0]
    halves = cache_rope.reshape(rows, 2, block_len // 2, -1)
    return halves.transpose(0, 2, 1, 3).reshape(rows, block_len // 2, -1)


def project_queries(nope_ref, rope_ref, uk_ref, qfull_ref, first, end):
    head_count, head_dim, latent = uk_ref.shape
    groups = qfull_ref.shape[0]
    size = qfull_ref.shape[1] // head_count
    half = LANES // 2

    def one_pair(pair, carry):
        slab = rope_ref[:, pl.ds(pl.multiple_of(pair * LANES, LANES), LANES)].astype(jnp.float32)
        turned = pltpu.roll(slab, half, 1)
        low = lax.broadcasted_iota(jnp.int32, slab.shape, 1) < half
        twice = (jnp.where(low, slab, turned), jnp.where(low, turned, slab))
        for odd in range(2):
            head = pair * 2 + odd
            query = nope_ref[:, pl.ds(pl.multiple_of(head * head_dim, LANES), head_dim)]
            lat = jnp.dot(query, uk_ref[head], preferred_element_type=jnp.float32)
            lat = lat.astype(jnp.bfloat16).reshape(groups, size, latent)
            rot = twice[odd].astype(jnp.bfloat16).reshape(groups, size, LANES)
            at = pl.ds(pl.multiple_of(head * size, size), size)
            qfull_ref[:, at, :latent] = lat
            qfull_ref[:, at, latent:] = rot
        return carry

    lax.fori_loop(first, end, one_pair, 0)


def query_kernel(nope_ref, rope_ref, uk_ref, qfull_ref):
    project_queries(nope_ref, rope_ref, uk_ref, qfull_ref, 0, uk_ref.shape[0] // 2)


def order_lists(sel_ref, owner_ref, order_ref, owners, cache_rows, late_owner, first_pos, size, block_len):
    groups, picks = sel_ref.shape
    sel = sel_ref[...]
    lane = lax.broadcasted_iota(jnp.int32, (groups, picks), 1)

    def find(b, found):
        return jnp.where(sel == b, owner_ref[b], found)

    owner = lax.fori_loop(0, owner_ref.shape[0], find, jnp.zeros_like(sel))
    row = owner * cache_rows + sel // owners
    key = jnp.where(lane == 0, 2 * picks, jnp.where(owner == late_owner, picks, 0)) + lane
    rank = jnp.zeros_like(sel)
    for j in range(picks):
        rank = rank + (key[:, j:j + 1] < key).astype(jnp.int32)
    wide = lax.broadcasted_iota(jnp.int32, (groups, LANES), 1)
    placed = jnp.zeros((groups, LANES), jnp.int32)
    for j in range(picks):
        placed = placed + jnp.where(rank[:, j:j + 1] == wide, row[:, j:j + 1], 0)
    at = lax.broadcasted_iota(jnp.int32, (groups, LANES), 0)
    behind = first_pos + at * size - sel[:, 0:1] * block_len
    order_ref[...] = jnp.where(wide == LANES - 1, behind, placed)


def fused_kernel(
    ctx_size, head_size, capacity, scale, owner_ref, sel_ref, lat_ref, krope_ref, nope_hbm, rope_hbm, uk_hbm, uv_hbm,
    out_ref, all_ref, late_ref, nope_ref, rope_ref, uk_ref, uv_ref, qfull_ref, scores, partial, peaks, totals,
    order_vec, order, local_sem, right_send, right_recv, left_send, left_recv, x_send, x_recv, z_core_send, z_core_recv,
    x_core_send, x_core_recv,
):
    ctx = lax.axis_index("ctx")
    head = lax.axis_index("head")
    across = (head + head_size // 2) % head_size
    sibling = head + 1 - 2 * (head % 2)
    sibling_across = (sibling + head_size // 2) % head_size
    rows, block_len, latent = lat_ref.shape
    quarter = rows // head_size
    piece = quarter // PIECES
    lane_groups = latent // LANES
    head_count, _, value_dim = uv_ref.shape
    groups, picks = sel_ref.shape
    size = qfull_ref.shape[1] // head_count
    has_left = ctx > 0
    has_right = ctx < ctx_size - 1
    last = ctx_size - 2

    barrier = pltpu.get_barrier_semaphore()
    pl.semaphore_signal(barrier, inc=1, device_id={"head": across}, device_id_type=MESH)
    pl.semaphore_signal(barrier, inc=1, device_id={"head": sibling}, device_id_type=MESH)

    @pl.when(has_left)
    def _():
        pl.semaphore_signal(barrier, inc=1, device_id={"ctx": ctx - 1}, device_id_type=MESH)

    @pl.when(has_right)
    def _():
        pl.semaphore_signal(barrier, inc=1, device_id={"ctx": ctx + 1}, device_id_type=MESH)

    loads = [
        pltpu.make_async_copy(source, target, local_sem.at[at])
        for at, (source, target) in enumerate(
            ((nope_hbm, nope_ref), (rope_hbm, rope_ref), (uk_hbm, uk_ref), (uv_hbm, uv_ref))
        )
    ]
    for load in loads:
        load.start()

    def pack_row(row, carry):
        for group in range(lane_groups):
            all_ref[ctx * rows + row, group * block_len:(group + 1) * block_len, :] = lat_ref[
                row, :, group * LANES:(group + 1) * LANES
            ]
        all_ref[ctx * rows + row, lane_groups * block_len:, :] = krope_ref[row]
        return carry

    lax.fori_loop(0, rows, pack_row, 0)
    pl.semaphore_wait(barrier, 2 + has_left.astype(jnp.int32) + has_right.astype(jnp.int32))

    def place(shard, part, k, step):
        at = part * quarter + k * piece
        if step == last:
            return late_ref.at[pl.ds(at, piece)]
        return all_ref.at[pl.ds(shard * rows + at, piece)]

    def hop(source, target, send, recv, device):
        return pltpu.make_async_remote_copy(
            src_ref=source, dst_ref=target, send_sem=send, recv_sem=recv, device_id=device, device_id_type=MESH
        )

    def z_copy(side, shard, k, step):
        source = place(shard, head, k, step - 1)
        target = place(shard, head, k, step)
        at = step * PIECES + k
        if side == 0:
            return hop(source, target, right_send.at[at], right_recv.at[at], {"ctx": ctx + 1})
        return hop(source, target, left_send.at[at], left_recv.at[at], {"ctx": ctx - 1})

    def local_copy(side, shard, k, step, part, send, recv, device):
        ref = place(shard, part, k, step)
        at = step * PIECES + k
        return hop(ref, ref, send.at[side, at], recv.at[side, at], {"head": device})

    def x_copy(side, shard, k, step, part):
        return local_copy(side, shard, k, step, part, x_send, x_recv, across)

    def z_core_copy(side, shard, k, step, part):
        return local_copy(side, shard, k, step, part, z_core_send, z_core_recv, sibling)

    def x_core_copy(side, shard, k, step, part):
        return local_copy(side, shard, k, step, part, x_core_send, x_core_recv, sibling)

    def sides(step):
        return (
            (0, ctx - 1 - step, ctx - 1 - step >= 0, has_right),
            (1, ctx + 1 + step, ctx + 1 + step <= ctx_size - 1, has_left),
        )

    def start_own(k, carry):
        @pl.when(has_right)
        def _():
            z_copy(0, ctx, k, 0).start()

        @pl.when(has_left)
        def _():
            z_copy(1, ctx, k, 0).start()

        return carry

    def from_z(step, k):
        for side, shard, there, onward in sides(step):

            @pl.when(there)
            def _(side=side, shard=shard, onward=onward):
                z_copy(side, shard, k, step).wait_recv()
                if step < last:

                    @pl.when(onward)
                    def _():
                        z_copy(side, shard, k, step + 1).start()

                x_copy(side, shard, k, step, head).start()
                z_core_copy(side, shard, k, step, head).start()

    def from_x(step, k):
        for side, shard, there, onward in sides(step):

            @pl.when(there)
            def _(side=side, shard=shard):
                x_copy(side, shard, k, step, across).wait_recv()
                x_core_copy(side, shard, k, step, across).start()

    def from_core(step, k):
        for side, shard, there, onward in sides(step):

            @pl.when(there)
            def _(side=side, shard=shard):
                z_core_copy(side, shard, k, step, sibling).wait_recv()
                x_core_copy(side, shard, k, step, sibling_across).wait_recv()

    lax.fori_loop(0, PIECES, start_own, 0)
    position = owner_ref.shape[0] * block_len - groups * size * ctx_size + ctx * groups * size
    late_owner = jnp.where(has_left & has_right, -1, ctx_size - 1 - ctx)
    order_lists(sel_ref, owner_ref, order_vec, ctx_size, rows, late_owner, position, size, block_len)
    to_scalar = pltpu.make_async_copy(order_vec, order, local_sem.at[4])
    to_scalar.start()
    for load in loads[:3]:
        load.wait()
    pairs = head_count // 2
    early_events = max(1, last * PIECES)
    share = -(-pairs // early_events)

    def project(at):
        project_queries(
            nope_ref, rope_ref, uk_ref, qfull_ref,
            jnp.minimum(at * share, pairs), jnp.minimum((at + 1) * share, pairs),
        )

    if last == 0:
        project(0)

    def run_step(step, with_project):
        def event(k, carry):
            from_z(step, k)
            if with_project:
                project(step * PIECES + k)

            @pl.when(k > 0)
            def _():
                from_x(step, k - 1)

            return carry

        lax.fori_loop(0, PIECES, event, 0)

    for step in range(last):
        if step > 0:
            from_x(step - 1, PIECES - 1)
        run_step(step, True)
    if last > 0:
        from_x(last - 1, PIECES - 1)

    def settle(step):
        lax.fori_loop(0, PIECES, lambda k, carry: (from_core(step, k), carry)[1], 0)

    for step in range(last):
        settle(step)
    to_scalar.wait()

    chunk = 4
    early = (picks - min(capacity, rows) - 1) // chunk * chunk if last > 0 else 0
    factor = scale * math.log2(math.e)

    def lists(first, count, final, service):
        def one_list(g, carry):
            block_rows = [order[g, first + j] for j in range(count)]
            query_at = lax.broadcasted_iota(jnp.int32, (qfull_ref.shape[1], LANES), 0) % size
            limit = order[g, LANES - 1] + query_at if final else None
            before = None if first == 0 else (peaks, totals, partial)
            peak, total, value = attend_part(
                g, before, block_rows, limit, qfull_ref, all_ref, scores, factor, block_len, latent, chunk
            )
            if final:
                found = value / jnp.sum(total, axis=1, keepdims=True)
                qfull_ref[g, :, :latent] = found.astype(jnp.bfloat16)
            else:
                peaks[g] = jnp.broadcast_to(peak, peaks.shape[1:])
                totals[g] = total
                partial[g] = value
            if service:
                every = max(1, groups // 2)

                @pl.when((g + 1) % every == 0)
                def _():
                    k = (g + 1) // every - 1

                    @pl.when(k < PIECES)
                    def _():
                        from_z(last, k)

                        @pl.when(k > 0)
                        def _():
                            from_x(last, k - 1)

            return carry

        lax.fori_loop(0, groups, one_list, 0)

    served = 0
    if early > 0:
        lists(0, early, False, True)
        served = min(PIECES, groups // max(1, groups // 2))

    def tail_event(k, carry):
        from_z(last, k)

        @pl.when(k > 0)
        def _():
            from_x(last, k - 1)

        return carry

    lax.fori_loop(served, PIECES, tail_event, 0)
    from_x(last, PIECES - 1)
    settle(last)

    @pl.when(late_owner >= 0)
    def _():
        def move(row, carry):
            all_ref[late_owner * rows + row] = late_ref[row]
            return carry

        lax.fori_loop(0, rows, move, 0)

    lists(early, picks - early, True, False)
    loads[3].wait()

    def one_head(h, carry):
        part = qfull_ref[:, pl.ds(pl.multiple_of(h * size, size), size), :latent].reshape(groups * size, latent)
        result = jnp.dot(part, uv_ref[h], preferred_element_type=jnp.float32)
        out_ref[:, pl.ds(pl.multiple_of(h * value_dim, LANES), value_dim)] = result.astype(jnp.bfloat16)
        return carry

    lax.fori_loop(0, head_count, one_head, 0)

    def finish(k, carry):
        @pl.when(has_right)
        def _():
            z_copy(0, ctx, k, 0).wait_send()

        @pl.when(has_left)
        def _():
            z_copy(1, ctx, k, 0).wait_send()

        for step in range(ctx_size - 1):
            for side, shard, there, onward in sides(step):

                @pl.when(there)
                def _(side=side, shard=shard, onward=onward, step=step):
                    x_copy(side, shard, k, step, head).wait_send()
                    z_core_copy(side, shard, k, step, head).wait_send()
                    x_core_copy(side, shard, k, step, across).wait_send()
                    if step < last:

                        @pl.when(onward)
                        def _():
                            z_copy(side, shard, k, step + 1).wait_send()

        return carry

    lax.fori_loop(0, PIECES, finish, 0)


def attend_part(g, before, block_rows, limit, qfull_ref, keys_ref, scores_ref, factor, block_len, latent, chunk):
    lane_groups = latent // LANES
    size = qfull_ref.shape[1]
    half = block_len // 2
    low = lax.broadcasted_iota(jnp.int32, (half, LANES), 1) < LANES // 2

    def values_of(row):
        return [
            keys_ref[row, group * block_len:(group + 1) * block_len, :] for group in range(lane_groups)
        ]

    def keys_of(row):
        rope = keys_ref[row, lane_groups * block_len:, :]
        zero = jnp.zeros_like(rope)
        both = jnp.concatenate([jnp.where(low, rope, zero), jnp.where(low, zero, rope)], axis=0)
        return values_of(row) + [both]

    def stack(rows, parts_of):
        return jnp.concatenate([jnp.concatenate(parts_of(row), axis=1) for row in rows], axis=0)

    width = chunk * block_len
    count = len(block_rows) // chunk
    query = qfull_ref[g]
    top = None
    for c in range(count):
        keys = stack(block_rows[c * chunk:(c + 1) * chunk], keys_of)
        score = lax.dot_general(query, keys, (((1,), (1,)), ((), ())), preferred_element_type=jnp.float32)
        if limit is not None and c == count - 1:
            end_part = score[:, width - LANES:]
            token = lax.broadcasted_iota(jnp.int32, end_part.shape, 1) - (LANES - block_len)
            end_part = jnp.where(token > limit, -jnp.inf, end_part)
            end_part = jnp.where(token < 0, score[:, width - LANES:], end_part)
            score = jnp.concatenate([score[:, :width - LANES], end_part], axis=1)
        scores_ref[:, c * width:(c + 1) * width] = score
        for at in range(width // LANES):
            piece = score[:, at * LANES:(at + 1) * LANES]
            top = piece if top is None else jnp.maximum(top, piece)
    peak = jnp.max(top, axis=1, keepdims=True)
    if before is None:
        total = jnp.zeros((size, LANES), jnp.float32)
        out = None
    else:
        peaks, totals, partial = before
        old = peaks[g][:, :1]
        peak = jnp.maximum(peak, old)
        fade = jnp.exp2((old - peak) * factor)
        total = totals[g] * fade
        out = partial[g] * fade
    shift = peak * factor
    for c in range(count):
        weight = jnp.exp2(scores_ref[:, c * width:(c + 1) * width] * factor - shift)
        for at in range(width // LANES):
            total = total + weight[:, at * LANES:(at + 1) * LANES]
        values = stack(block_rows[c * chunk:(c + 1) * chunk], values_of)
        more = jnp.dot(weight.astype(jnp.bfloat16), values, preferred_element_type=jnp.float32)
        out = more if out is None else out + more
    return peak, total, out


def attend(block_rows, limit, q_ref, keys_ref, scores_ref, scale, block_len, latent, chunk):
    lane_groups = latent // LANES
    size = q_ref.shape[0]
    half = block_len // 2
    low = lax.broadcasted_iota(jnp.int32, (half, LANES), 1) < LANES // 2

    def values_of(row):
        return [
            keys_ref[row, group * block_len:(group + 1) * block_len, :] for group in range(lane_groups)
        ]

    def keys_of(row):
        rope = keys_ref[row, lane_groups * block_len:, :]
        zero = jnp.zeros_like(rope)
        both = jnp.concatenate([jnp.where(low, rope, zero), jnp.where(low, zero, rope)], axis=0)
        return values_of(row) + [both]

    def stack(rows, parts_of):
        return jnp.concatenate([jnp.concatenate(parts_of(row), axis=1) for row in rows], axis=0)

    width = chunk * block_len
    count = len(block_rows) // chunk
    query = q_ref[...]
    top = None
    for c in range(count):
        keys = stack(block_rows[c * chunk:(c + 1) * chunk], keys_of)
        score = lax.dot_general(query, keys, (((1,), (1,)), ((), ())), preferred_element_type=jnp.float32)
        if c == 0:
            head_part = score[:, :LANES]
            lane = lax.broadcasted_iota(jnp.int32, head_part.shape, 1)
            barred = (lane < block_len) & (lane > limit)
            score = jnp.concatenate([jnp.where(barred, -jnp.inf, head_part), score[:, LANES:]], axis=1)
        scores_ref[:, c * width:(c + 1) * width] = score
        for at in range(width // LANES):
            part = score[:, at * LANES:(at + 1) * LANES]
            top = part if top is None else jnp.maximum(top, part)
    factor = scale * math.log2(math.e)
    shift = jnp.max(top, axis=1, keepdims=True) * factor
    total = jnp.zeros((size, LANES), jnp.float32)
    out = jnp.zeros((size, latent), jnp.float32)
    for c in range(count):
        weight = jnp.exp2(scores_ref[:, c * width:(c + 1) * width] * factor - shift)
        for at in range(width // LANES):
            total = total + weight[:, at * LANES:(at + 1) * LANES]
        values = stack(block_rows[c * chunk:(c + 1) * chunk], values_of)
        out = out + jnp.dot(weight.astype(jnp.bfloat16), values, preferred_element_type=jnp.float32)
    return out / jnp.sum(total, axis=1, keepdims=True)


def attention_kernel(
    scale, block_len, rows_ref, limit_ref, qfull_ref, keys_ref, uv_ref, out_ref, scores, out_latent
):
    head_count, latent, value_dim = uv_ref.shape
    groups = qfull_ref.shape[0]
    size = qfull_ref.shape[1] // head_count
    picks = rows_ref.shape[1]

    def one_list(g, carry):
        block_rows = [rows_ref[g, j] for j in range(picks)]
        query_at = lax.broadcasted_iota(jnp.int32, (qfull_ref.shape[1], LANES), 0) % size
        limit = limit_ref[g] + query_at
        found = attend(
            block_rows, limit, qfull_ref.at[g], keys_ref, scores, scale, block_len, latent, 4
        )
        out_latent[g] = found.astype(jnp.bfloat16)
        return carry

    lax.fori_loop(0, groups, one_list, 0)

    def one_head(h, carry):
        part = out_latent[:, pl.ds(pl.multiple_of(h * size, size), size), :].reshape(groups * size, latent)
        result = jnp.dot(part, uv_ref[h], preferred_element_type=jnp.float32)
        out_ref[:, pl.ds(pl.multiple_of(h * value_dim, LANES), value_dim)] = result.astype(jnp.bfloat16)
        return carry

    lax.fori_loop(0, head_count, one_head, 0)


def on_device(q_nope, q_rope, w_uk, w_uv, cache_latent, cache_rope, block_owner, selection):
    owners = lax.axis_size("ctx")
    heads = lax.axis_size("head")
    my_index = lax.axis_index("ctx")
    query_count = q_nope.shape[0]
    head_count, head_dim, latent = w_uk.shape
    value_dim = w_uv.shape[2]
    cache_rows, block_len = cache_latent.shape[:2]
    rope_dim = cache_rope.shape[1] // block_len
    group_count, pick_count = selection.shape
    block_count = block_owner.shape[0]
    query_blocks = query_count // block_len
    capacity = max(3 + query_blocks // 8, (2 * pick_count + 2 * query_blocks) // owners)
    group_size = query_count // group_count
    block_ids = lax.broadcasted_iota(jnp.int32, (block_count,), 0)
    rope_rows = split_rope(cache_rope, block_len)
    packed_rows = latent // LANES * block_len + block_len // 2
    qfull_shape = jax.ShapeDtypeStruct((group_count, head_count * group_size, latent + LANES), jnp.bfloat16)
    vmem = pl.BlockSpec(memory_space=pltpu.VMEM)
    smem = pl.BlockSpec(memory_space=pltpu.SMEM)

    out_shape = jax.ShapeDtypeStruct((query_count, head_count * value_dim), jnp.bfloat16)
    scale = (head_dim + rope_dim) ** (-0.5)

    if cache_rows <= 2 * capacity:
        events = (owners - 1) * PIECES
        width = head_count * group_size
        anywhere = pl.BlockSpec(memory_space=pl.ANY)
        return pl.pallas_call(
            functools.partial(fused_kernel, owners, heads, capacity, scale),
            out_shape=out_shape,
            in_specs=[smem, vmem, vmem, vmem] + [anywhere] * 4,
            out_specs=vmem,
            scratch_shapes=[
                pltpu.VMEM((owners * cache_rows, packed_rows, LANES), jnp.bfloat16),
                pltpu.VMEM((cache_rows, packed_rows, LANES), jnp.bfloat16),
                pltpu.VMEM(q_nope.shape, jnp.bfloat16),
                pltpu.VMEM(q_rope.shape, jnp.bfloat16),
                pltpu.VMEM(w_uk.shape, jnp.bfloat16),
                pltpu.VMEM(w_uv.shape, jnp.bfloat16),
                pltpu.VMEM(qfull_shape.shape, jnp.bfloat16),
                pltpu.VMEM((width, pick_count * block_len), jnp.float32),
                pltpu.VMEM((group_count, width, latent), jnp.float32),
                pltpu.VMEM((group_count, width, LANES), jnp.float32),
                pltpu.VMEM((group_count, width, LANES), jnp.float32),
                pltpu.VMEM((group_count, LANES), jnp.int32),
                pltpu.SMEM((group_count, LANES), jnp.int32),
                pltpu.SemaphoreType.DMA((5,)),
            ] + [pltpu.SemaphoreType.DMA((events,))] * 4 + [pltpu.SemaphoreType.DMA((2, events))] * 6,
            compiler_params=pltpu.CompilerParams(
                collective_id=0, has_side_effects=True, vmem_limit_bytes=VMEM_BYTES
            ),
        )(block_owner, selection, cache_latent, rope_rows, q_nope, q_rope, w_uk, w_uv)
    owner_ids = lax.broadcasted_iota(jnp.int32, (owners, block_count), 0)
    owned_all = (block_owner[None, :] == owner_ids).astype(jnp.int32)
    present = jnp.zeros((block_count,), jnp.int32).at[selection.reshape(-1)].set(1)
    listings, ranking = jax.vmap(lambda owned: slot_lists(present, owned, capacity, owners))(
        owned_all
    )
    position = block_owner * capacity + jnp.sum(ranking, axis=0)
    wanted = lax.all_to_all(listings, "ctx", split_axis=0, concat_axis=0, tiled=True)
    flat_rows = wanted.reshape(-1)
    asked = pack_blocks(cache_latent[flat_rows], rope_rows[flat_rows])
    asked = asked.reshape(owners, capacity, packed_rows, LANES)
    keys = lax.all_to_all(asked, "ctx", split_axis=0, concat_axis=0, tiled=True)
    keys = keys.reshape(owners * capacity, packed_rows, LANES)
    qfull = pl.pallas_call(
        query_kernel,
        out_shape=qfull_shape,
        in_specs=[vmem] * 3,
        out_specs=vmem,
        compiler_params=pltpu.CompilerParams(vmem_limit_bytes=VMEM_BYTES),
    )(q_nope, q_rope, w_uk)

    first_pos = block_count * block_len - query_count * owners + my_index * query_count
    limits = first_pos + jnp.arange(group_count, dtype=jnp.int32) * group_size - selection[:, 0] * block_len
    return pl.pallas_call(
        functools.partial(attention_kernel, scale, block_len),
        out_shape=out_shape,
        in_specs=[smem, smem, vmem, vmem, vmem],
        out_specs=vmem,
        scratch_shapes=[
            pltpu.VMEM((head_count * group_size, pick_count * block_len), jnp.float32),
            pltpu.VMEM((group_count, head_count * group_size, latent), jnp.bfloat16),
        ],
        compiler_params=pltpu.CompilerParams(vmem_limit_bytes=VMEM_BYTES),
    )(position[selection], limits, qfull, keys, w_uv)


def solution(mesh):
    return jax.shard_map(
        on_device,
        mesh=mesh,
        in_specs=(
            P(("groups", "ctx"), "head"),
            P(("groups", "ctx"), "head"),
            P("head", None, None),
            P("head", None, None),
            P(("groups", "ctx"), None, None),
            P(("groups", "ctx"), None),
            P("groups"),
            P(("groups", "ctx"), None),
        ),
        out_specs=P(("groups", "ctx"), "head"),
        check_vma=False,
    )
```

```python
import functools
import math

import jax
import jax.numpy as jnp
from jax import lax
from jax.experimental import pallas as pl
from jax.experimental.pallas import tpu as pltpu
from jax.sharding import PartitionSpec as P

LANES = 128
PIECES = 4
VMEM_BYTES = 56 * 1024 * 1024
MESH = pl.DeviceIdType.MESH


def slot_lists(present, owned, capacity, owners):
    member = present * owned
    ranking = jnp.cumsum(member) - 1
    local_row = lax.broadcasted_iota(jnp.int32, present.shape, 0) // owners
    slot_ids = lax.broadcasted_iota(jnp.int32, (capacity,) + present.shape, 0)
    matched = (ranking[None, :] == slot_ids) & (member[None, :] > 0)
    listing = jnp.sum(jnp.where(matched, local_row[None, :], 0), axis=1)
    return (listing, jnp.where(member > 0, ranking, 0))


def pack_blocks(latent_rows, rope_rows):
    rows, block_len, latent = latent_rows.shape
    lat = latent_rows.reshape(rows, block_len, latent // LANES, LANES)
    lat = lat.transpose(0, 2, 1, 3).reshape(rows, -1, LANES)
    return jnp.concatenate([lat, rope_rows], axis=1)


def split_rope(cache_rope, block_len):
    rows = cache_rope.shape[0]
    halves = cache_rope.reshape(rows, 2, block_len // 2, -1)
    return halves.transpose(0, 2, 1, 3).reshape(rows, block_len // 2, -1)


def project_queries(nope_ref, rope_ref, uk_ref, qfull_ref, first, end):
    head_count, head_dim, latent = uk_ref.shape
    groups = qfull_ref.shape[0]
    size = qfull_ref.shape[1] // head_count
    half = LANES // 2

    def one_pair(pair, carry):
        slab = rope_ref[:, pl.ds(pl.multiple_of(pair * LANES, LANES), LANES)].astype(jnp.float32)
        turned = pltpu.roll(slab, half, 1)
        low = lax.broadcasted_iota(jnp.int32, slab.shape, 1) < half
        twice = (jnp.where(low, slab, turned), jnp.where(low, turned, slab))
        for odd in range(2):
            head = pair * 2 + odd
            query = nope_ref[:, pl.ds(pl.multiple_of(head * head_dim, LANES), head_dim)]
            lat = jnp.dot(query, uk_ref[head], preferred_element_type=jnp.float32)
            lat = lat.astype(jnp.bfloat16).reshape(groups, size, latent)
            rot = twice[odd].astype(jnp.bfloat16).reshape(groups, size, LANES)
            at = pl.ds(pl.multiple_of(head * size, size), size)
            qfull_ref[:, at, :latent] = lat
            qfull_ref[:, at, latent:] = rot
        return carry

    lax.fori_loop(first, end, one_pair, 0)


def query_kernel(nope_ref, rope_ref, uk_ref, qfull_ref):
    project_queries(nope_ref, rope_ref, uk_ref, qfull_ref, 0, uk_ref.shape[0] // 2)


def order_lists(sel_ref, owner_ref, order_ref, owners, cache_rows, late_owner, first_pos, size, block_len):
    groups, picks = sel_ref.shape
    sel = sel_ref[...]
    lane = lax.broadcasted_iota(jnp.int32, (groups, picks), 1)

    def find(b, found):
        return jnp.where(sel == b, owner_ref[b], found)

    owner = lax.fori_loop(0, owner_ref.shape[0], find, jnp.zeros_like(sel))
    row = owner * cache_rows + sel // owners
    key = jnp.where(lane == 0, 2 * picks, jnp.where(owner == late_owner, picks, 0)) + lane
    rank = jnp.zeros_like(sel)
    for j in range(picks):
        rank = rank + (key[:, j:j + 1] < key).astype(jnp.int32)
    wide = lax.broadcasted_iota(jnp.int32, (groups, LANES), 1)
    placed = jnp.zeros((groups, LANES), jnp.int32)
    for j in range(picks):
        placed = placed + jnp.where(rank[:, j:j + 1] == wide, row[:, j:j + 1], 0)
    at = lax.broadcasted_iota(jnp.int32, (groups, LANES), 0)
    behind = first_pos + at * size - sel[:, 0:1] * block_len
    order_ref[...] = jnp.where(wide == LANES - 1, behind, placed)


def fused_kernel(
    ctx_size, head_size, capacity, scale, owner_ref, sel_ref, lat_ref, krope_ref, nope_hbm, rope_hbm, uk_hbm, uv_hbm,
    out_ref, all_ref, late_ref, nope_ref, rope_ref, uk_ref, uv_ref, qfull_ref, found_ref, scores, more_scores, partial, peaks, totals, fades,
    order_vec, order, local_sem, right_send, right_recv, left_send, left_recv, x_send, x_recv, z_core_send, z_core_recv,
    x_core_send, x_core_recv,
):
    ctx = lax.axis_index("ctx")
    head = lax.axis_index("head")
    across = (head + head_size // 2) % head_size
    sibling = head + 1 - 2 * (head % 2)
    sibling_across = (sibling + head_size // 2) % head_size
    rows, block_len, latent = lat_ref.shape
    quarter = rows // head_size
    piece = quarter // PIECES
    lane_groups = latent // LANES
    head_count, _, value_dim = uv_ref.shape
    groups, picks = sel_ref.shape
    size = qfull_ref.shape[1] // head_count
    has_left = ctx > 0
    has_right = ctx < ctx_size - 1
    last = ctx_size - 2

    barrier = pltpu.get_barrier_semaphore()
    pl.semaphore_signal(barrier, inc=1, device_id={"head": across}, device_id_type=MESH)
    pl.semaphore_signal(barrier, inc=1, device_id={"head": sibling}, device_id_type=MESH)

    @pl.when(has_left)
    def _():
        pl.semaphore_signal(barrier, inc=1, device_id={"ctx": ctx - 1}, device_id_type=MESH)

    @pl.when(has_right)
    def _():
        pl.semaphore_signal(barrier, inc=1, device_id={"ctx": ctx + 1}, device_id_type=MESH)

    loads = [
        pltpu.make_async_copy(source, target, local_sem.at[at])
        for at, (source, target) in enumerate(
            ((nope_hbm, nope_ref), (rope_hbm, rope_ref), (uk_hbm, uk_ref), (uv_hbm, uv_ref))
        )
    ]
    for load in loads:
        load.start()

    def pack_row(row, carry):
        for group in range(lane_groups):
            all_ref[ctx * rows + row, group * block_len:(group + 1) * block_len, :] = lat_ref[
                row, :, group * LANES:(group + 1) * LANES
            ]
        all_ref[ctx * rows + row, lane_groups * block_len:, :] = krope_ref[row]
        return carry

    lax.fori_loop(0, rows, pack_row, 0)
    pl.semaphore_wait(barrier, 2 + has_left.astype(jnp.int32) + has_right.astype(jnp.int32))

    def place(shard, part, k, step):
        at = part * quarter + k * piece
        if step == last:
            return late_ref.at[pl.ds(at, piece)]
        return all_ref.at[pl.ds(shard * rows + at, piece)]

    def hop(source, target, send, recv, device):
        return pltpu.make_async_remote_copy(
            src_ref=source, dst_ref=target, send_sem=send, recv_sem=recv, device_id=device, device_id_type=MESH
        )

    def z_copy(side, shard, k, step):
        source = place(shard, head, k, step - 1)
        target = place(shard, head, k, step)
        at = step * PIECES + k
        if side == 0:
            return hop(source, target, right_send.at[at], right_recv.at[at], {"ctx": ctx + 1})
        return hop(source, target, left_send.at[at], left_recv.at[at], {"ctx": ctx - 1})

    def local_copy(side, shard, k, step, part, send, recv, device):
        ref = place(shard, part, k, step)
        at = step * PIECES + k
        return hop(ref, ref, send.at[side, at], recv.at[side, at], {"head": device})

    def x_copy(side, shard, k, step, part):
        return local_copy(side, shard, k, step, part, x_send, x_recv, across)

    def z_core_copy(side, shard, k, step, part):
        return local_copy(side, shard, k, step, part, z_core_send, z_core_recv, sibling)

    def x_core_copy(side, shard, k, step, part):
        return local_copy(side, shard, k, step, part, x_core_send, x_core_recv, sibling)

    def sides(step):
        return (
            (0, ctx - 1 - step, ctx - 1 - step >= 0, has_right),
            (1, ctx + 1 + step, ctx + 1 + step <= ctx_size - 1, has_left),
        )

    def start_own(k, carry):
        @pl.when(has_right)
        def _():
            z_copy(0, ctx, k, 0).start()

        @pl.when(has_left)
        def _():
            z_copy(1, ctx, k, 0).start()

        return carry

    def from_z(step, k):
        for side, shard, there, onward in sides(step):

            @pl.when(there)
            def _(side=side, shard=shard, onward=onward):
                z_copy(side, shard, k, step).wait_recv()
                if step < last:

                    @pl.when(onward)
                    def _():
                        z_copy(side, shard, k, step + 1).start()

                x_copy(side, shard, k, step, head).start()
                z_core_copy(side, shard, k, step, head).start()

    def from_x(step, k):
        for side, shard, there, onward in sides(step):

            @pl.when(there)
            def _(side=side, shard=shard):
                x_copy(side, shard, k, step, across).wait_recv()
                x_core_copy(side, shard, k, step, across).start()

    def from_core(step, k):
        for side, shard, there, onward in sides(step):

            @pl.when(there)
            def _(side=side, shard=shard):
                z_core_copy(side, shard, k, step, sibling).wait_recv()
                x_core_copy(side, shard, k, step, sibling_across).wait_recv()

    lax.fori_loop(0, PIECES, start_own, 0)
    position = owner_ref.shape[0] * block_len - groups * size * ctx_size + ctx * groups * size
    late_owner = jnp.where(has_left & has_right, -1, ctx_size - 1 - ctx)
    order_lists(sel_ref, owner_ref, order_vec, ctx_size, rows, late_owner, position, size, block_len)
    to_scalar = pltpu.make_async_copy(order_vec, order, local_sem.at[4])
    to_scalar.start()
    for load in loads[:3]:
        load.wait()
    pairs = head_count // 2
    early_events = max(1, last * PIECES)
    share = -(-pairs // early_events)

    def project(at):
        project_queries(
            nope_ref, rope_ref, uk_ref, qfull_ref,
            jnp.minimum(at * share, pairs), jnp.minimum((at + 1) * share, pairs),
        )

    if last == 0:
        project(0)

    def run_step(step, with_project):
        def event(k, carry):
            from_z(step, k)
            if with_project:
                project(step * PIECES + k)

            @pl.when(k > 0)
            def _():
                from_x(step, k - 1)

            return carry

        lax.fori_loop(0, PIECES, event, 0)

    for step in range(last):
        if step > 0:
            from_x(step - 1, PIECES - 1)
        run_step(step, True)
    if last > 0:
        from_x(last - 1, PIECES - 1)

    def settle(step):
        lax.fori_loop(0, PIECES, lambda k, carry: (from_core(step, k), carry)[1], 0)

    for step in range(last):
        settle(step)
    to_scalar.wait()

    chunk = 4
    early = (picks - min(capacity, rows) - 1) // chunk * chunk if last > 0 else 0
    factor = scale * math.log2(math.e)

    def lists(first, count, final, service):
        steps = count // chunk
        query_at = lax.broadcasted_iota(jnp.int32, (qfull_ref.shape[1], LANES), 0) % size

        def rows_of(g):
            return [order[g, first + j] for j in range(count)]

        def limit_of(g):
            return order[g, LANES - 1] + query_at if final else None

        def store_top(g, top):
            peak = jnp.max(top, axis=1, keepdims=True)
            if first > 0:
                old = peaks[g]
                peak = jnp.maximum(peak, old[:, :1])
                fades[...] = jnp.exp2((old - peak) * factor)
            peaks[g] = jnp.broadcast_to(peak, peaks.shape[1:])

        def score(g, buffer):
            block_rows = rows_of(g)
            top = None
            for c in range(steps):
                top = score_step(
                    g, block_rows, limit_of(g), c, qfull_ref, all_ref, buffer, block_len, latent, chunk, top
                )
            store_top(g, top)

        def both(g, buffer, then, then_buffer):
            block_rows = rows_of(g)
            shift = peaks[g][:, :1] * factor
            if first > 0:
                fade = fades[:, :1]
                total, value = totals[g] * fade, partial[g] * fade
            else:
                total, value = jnp.zeros(totals.shape[1:], jnp.float32), None
            then_rows = None if then is None else rows_of(then)
            top = None
            for c in range(steps):
                if then is not None:
                    top = score_step(
                        then, then_rows, limit_of(then), c, qfull_ref, all_ref, then_buffer, block_len, latent,
                        chunk, top,
                    )
                total, value = weigh_step(
                    block_rows, c, all_ref, buffer, factor, shift, block_len, latent, chunk, total, value
                )
            if final:
                found = value / jnp.sum(total, axis=1, keepdims=True)
                found_ref[g] = found.astype(jnp.bfloat16)
            else:
                totals[g] = total
                partial[g] = value
            if then is not None:
                store_top(then, top)

        def serve(k):
            from_z(last, k)

            @pl.when(k > 0)
            def _():
                from_x(last, k - 1)

        score(0, scores)

        def two_lists(pair, carry):
            both(2 * pair, scores, 2 * pair + 1, more_scores)

            @pl.when(pair < groups // 2 - 1)
            def _():
                both(2 * pair + 1, more_scores, 2 * pair + 2, scores)

            @pl.when(pair == groups // 2 - 1)
            def _():
                both(2 * pair + 1, more_scores, None, None)

            if service:

                @pl.when((pair == 1) | (pair == 3))
                def _():
                    serve(pair // 2)

            return carry

        lax.fori_loop(0, groups // 2, two_lists, 0)

    served = 0
    if early > 0:
        lists(0, early, False, True)
        served = groups // 4

    def tail_event(k, carry):
        from_z(last, k)

        @pl.when(k > 0)
        def _():
            from_x(last, k - 1)

        return carry

    lax.fori_loop(served, PIECES, tail_event, 0)
    from_x(last, PIECES - 1)
    settle(last)

    @pl.when(late_owner >= 0)
    def _():
        def move(row, carry):
            all_ref[late_owner * rows + row] = late_ref[row]
            return carry

        lax.fori_loop(0, rows, move, 0)

    lists(early, picks - early, True, False)
    loads[3].wait()

    def one_head(h, carry):
        part = found_ref[:, pl.ds(pl.multiple_of(h * size, size), size), :].reshape(groups * size, latent)
        result = jnp.dot(part, uv_ref[h], preferred_element_type=jnp.float32)
        out_ref[:, pl.ds(pl.multiple_of(h * value_dim, LANES), value_dim)] = result.astype(jnp.bfloat16)
        return carry

    lax.fori_loop(0, head_count, one_head, 0)

    def finish(k, carry):
        @pl.when(has_right)
        def _():
            z_copy(0, ctx, k, 0).wait_send()

        @pl.when(has_left)
        def _():
            z_copy(1, ctx, k, 0).wait_send()

        for step in range(ctx_size - 1):
            for side, shard, there, onward in sides(step):

                @pl.when(there)
                def _(side=side, shard=shard, onward=onward, step=step):
                    x_copy(side, shard, k, step, head).wait_send()
                    z_core_copy(side, shard, k, step, head).wait_send()
                    x_core_copy(side, shard, k, step, across).wait_send()
                    if step < last:

                        @pl.when(onward)
                        def _():
                            z_copy(side, shard, k, step + 1).wait_send()

        return carry

    lax.fori_loop(0, PIECES, finish, 0)


def score_step(g, block_rows, limit, c, qfull_ref, keys_ref, scores_ref, block_len, latent, chunk, top):
    lane_groups = latent // LANES
    half = block_len // 2
    low = lax.broadcasted_iota(jnp.int32, (half, LANES), 1) < LANES // 2
    width = chunk * block_len

    def keys_of(row):
        rope = keys_ref[row, lane_groups * block_len:, :]
        zero = jnp.zeros_like(rope)
        both = jnp.concatenate([jnp.where(low, rope, zero), jnp.where(low, zero, rope)], axis=0)
        parts = [keys_ref[row, group * block_len:(group + 1) * block_len, :] for group in range(lane_groups)]
        return jnp.concatenate(parts + [both], axis=1)

    keys = jnp.concatenate([keys_of(row) for row in block_rows[c * chunk:(c + 1) * chunk]], axis=0)
    score = lax.dot_general(
        qfull_ref[g], keys, (((1,), (1,)), ((), ())), preferred_element_type=jnp.float32
    )
    if limit is not None and (c + 1) * chunk == len(block_rows):
        end_part = score[:, width - LANES:]
        token = lax.broadcasted_iota(jnp.int32, end_part.shape, 1) - (LANES - block_len)
        end_part = jnp.where((token >= 0) & (token > limit), -jnp.inf, end_part)
        score = jnp.concatenate([score[:, :width - LANES], end_part], axis=1)
    scores_ref[:, c * width:(c + 1) * width] = score
    for at in range(width // LANES):
        piece = score[:, at * LANES:(at + 1) * LANES]
        top = piece if top is None else jnp.maximum(top, piece)
    return top


def weigh_step(block_rows, c, keys_ref, scores_ref, factor, shift, block_len, latent, chunk, total, out):
    lane_groups = latent // LANES
    width = chunk * block_len

    def values_of(row):
        parts = [keys_ref[row, group * block_len:(group + 1) * block_len, :] for group in range(lane_groups)]
        return jnp.concatenate(parts, axis=1)

    weight = jnp.exp2(scores_ref[:, c * width:(c + 1) * width] * factor - shift)
    for at in range(width // LANES):
        total = total + weight[:, at * LANES:(at + 1) * LANES]
    values = jnp.concatenate([values_of(row) for row in block_rows[c * chunk:(c + 1) * chunk]], axis=0)
    more = jnp.dot(weight.astype(jnp.bfloat16), values, preferred_element_type=jnp.float32)
    return total, more if out is None else out + more


def attend(block_rows, limit, q_ref, keys_ref, scores_ref, scale, block_len, latent, chunk):
    lane_groups = latent // LANES
    size = q_ref.shape[0]
    half = block_len // 2
    low = lax.broadcasted_iota(jnp.int32, (half, LANES), 1) < LANES // 2

    def values_of(row):
        return [
            keys_ref[row, group * block_len:(group + 1) * block_len, :] for group in range(lane_groups)
        ]

    def keys_of(row):
        rope = keys_ref[row, lane_groups * block_len:, :]
        zero = jnp.zeros_like(rope)
        both = jnp.concatenate([jnp.where(low, rope, zero), jnp.where(low, zero, rope)], axis=0)
        return values_of(row) + [both]

    def stack(rows, parts_of):
        return jnp.concatenate([jnp.concatenate(parts_of(row), axis=1) for row in rows], axis=0)

    width = chunk * block_len
    count = len(block_rows) // chunk
    query = q_ref[...]
    top = None
    for c in range(count):
        keys = stack(block_rows[c * chunk:(c + 1) * chunk], keys_of)
        score = lax.dot_general(query, keys, (((1,), (1,)), ((), ())), preferred_element_type=jnp.float32)
        if c == 0:
            head_part = score[:, :LANES]
            lane = lax.broadcasted_iota(jnp.int32, head_part.shape, 1)
            barred = (lane < block_len) & (lane > limit)
            score = jnp.concatenate([jnp.where(barred, -jnp.inf, head_part), score[:, LANES:]], axis=1)
        scores_ref[:, c * width:(c + 1) * width] = score
        for at in range(width // LANES):
            part = score[:, at * LANES:(at + 1) * LANES]
            top = part if top is None else jnp.maximum(top, part)
    factor = scale * math.log2(math.e)
    shift = jnp.max(top, axis=1, keepdims=True) * factor
    total = jnp.zeros((size, LANES), jnp.float32)
    out = jnp.zeros((size, latent), jnp.float32)
    for c in range(count):
        weight = jnp.exp2(scores_ref[:, c * width:(c + 1) * width] * factor - shift)
        for at in range(width // LANES):
            total = total + weight[:, at * LANES:(at + 1) * LANES]
        values = stack(block_rows[c * chunk:(c + 1) * chunk], values_of)
        out = out + jnp.dot(weight.astype(jnp.bfloat16), values, preferred_element_type=jnp.float32)
    return out / jnp.sum(total, axis=1, keepdims=True)


def attention_kernel(
    scale, block_len, rows_ref, limit_ref, qfull_ref, keys_ref, uv_ref, out_ref, scores, out_latent
):
    head_count, latent, value_dim = uv_ref.shape
    groups = qfull_ref.shape[0]
    size = qfull_ref.shape[1] // head_count
    picks = rows_ref.shape[1]

    def one_list(g, carry):
        block_rows = [rows_ref[g, j] for j in range(picks)]
        query_at = lax.broadcasted_iota(jnp.int32, (qfull_ref.shape[1], LANES), 0) % size
        limit = limit_ref[g] + query_at
        found = attend(
            block_rows, limit, qfull_ref.at[g], keys_ref, scores, scale, block_len, latent, 4
        )
        out_latent[g] = found.astype(jnp.bfloat16)
        return carry

    lax.fori_loop(0, groups, one_list, 0)

    def one_head(h, carry):
        part = out_latent[:, pl.ds(pl.multiple_of(h * size, size), size), :].reshape(groups * size, latent)
        result = jnp.dot(part, uv_ref[h], preferred_element_type=jnp.float32)
        out_ref[:, pl.ds(pl.multiple_of(h * value_dim, LANES), value_dim)] = result.astype(jnp.bfloat16)
        return carry

    lax.fori_loop(0, head_count, one_head, 0)


def on_device(q_nope, q_rope, w_uk, w_uv, cache_latent, cache_rope, block_owner, selection):
    owners = lax.axis_size("ctx")
    heads = lax.axis_size("head")
    my_index = lax.axis_index("ctx")
    query_count = q_nope.shape[0]
    head_count, head_dim, latent = w_uk.shape
    value_dim = w_uv.shape[2]
    cache_rows, block_len = cache_latent.shape[:2]
    rope_dim = cache_rope.shape[1] // block_len
    group_count, pick_count = selection.shape
    block_count = block_owner.shape[0]
    query_blocks = query_count // block_len
    capacity = max(3 + query_blocks // 8, (2 * pick_count + 2 * query_blocks) // owners)
    group_size = query_count // group_count
    block_ids = lax.broadcasted_iota(jnp.int32, (block_count,), 0)
    rope_rows = split_rope(cache_rope, block_len)
    packed_rows = latent // LANES * block_len + block_len // 2
    qfull_shape = jax.ShapeDtypeStruct((group_count, head_count * group_size, latent + LANES), jnp.bfloat16)
    vmem = pl.BlockSpec(memory_space=pltpu.VMEM)
    smem = pl.BlockSpec(memory_space=pltpu.SMEM)

    out_shape = jax.ShapeDtypeStruct((query_count, head_count * value_dim), jnp.bfloat16)
    scale = (head_dim + rope_dim) ** (-0.5)

    if cache_rows <= 2 * capacity:
        events = (owners - 1) * PIECES
        width = head_count * group_size
        anywhere = pl.BlockSpec(memory_space=pl.ANY)
        return pl.pallas_call(
            functools.partial(fused_kernel, owners, heads, capacity, scale),
            out_shape=out_shape,
            in_specs=[smem, vmem, vmem, vmem] + [anywhere] * 4,
            out_specs=vmem,
            scratch_shapes=[
                pltpu.VMEM((owners * cache_rows, packed_rows, LANES), jnp.bfloat16),
                pltpu.VMEM((cache_rows, packed_rows, LANES), jnp.bfloat16),
                pltpu.VMEM(q_nope.shape, jnp.bfloat16),
                pltpu.VMEM(q_rope.shape, jnp.bfloat16),
                pltpu.VMEM(w_uk.shape, jnp.bfloat16),
                pltpu.VMEM(w_uv.shape, jnp.bfloat16),
                pltpu.VMEM(qfull_shape.shape, jnp.bfloat16),
                pltpu.VMEM((group_count, width, latent), jnp.bfloat16),
                pltpu.VMEM((width, pick_count * block_len), jnp.float32),
                pltpu.VMEM((width, pick_count * block_len), jnp.float32),
                pltpu.VMEM((group_count, width, latent), jnp.float32),
                pltpu.VMEM((group_count, width, LANES), jnp.float32),
                pltpu.VMEM((group_count, width, LANES), jnp.float32),
                pltpu.VMEM((width, LANES), jnp.float32),
                pltpu.VMEM((group_count, LANES), jnp.int32),
                pltpu.SMEM((group_count, LANES), jnp.int32),
                pltpu.SemaphoreType.DMA((5,)),
            ] + [pltpu.SemaphoreType.DMA((events,))] * 4 + [pltpu.SemaphoreType.DMA((2, events))] * 6,
            compiler_params=pltpu.CompilerParams(
                collective_id=0, has_side_effects=True, vmem_limit_bytes=VMEM_BYTES
            ),
        )(block_owner, selection, cache_latent, rope_rows, q_nope, q_rope, w_uk, w_uv)
    owner_ids = lax.broadcasted_iota(jnp.int32, (owners, block_count), 0)
    owned_all = (block_owner[None, :] == owner_ids).astype(jnp.int32)
    present = jnp.zeros((block_count,), jnp.int32).at[selection.reshape(-1)].set(1)
    listings, ranking = jax.vmap(lambda owned: slot_lists(present, owned, capacity, owners))(
        owned_all
    )
    position = block_owner * capacity + jnp.sum(ranking, axis=0)
    wanted = lax.all_to_all(listings, "ctx", split_axis=0, concat_axis=0, tiled=True)
    flat_rows = wanted.reshape(-1)
    asked = pack_blocks(cache_latent[flat_rows], rope_rows[flat_rows])
    asked = asked.reshape(owners, capacity, packed_rows, LANES)
    keys = lax.all_to_all(asked, "ctx", split_axis=0, concat_axis=0, tiled=True)
    keys = keys.reshape(owners * capacity, packed_rows, LANES)
    qfull = pl.pallas_call(
        query_kernel,
        out_shape=qfull_shape,
        in_specs=[vmem] * 3,
        out_specs=vmem,
        compiler_params=pltpu.CompilerParams(vmem_limit_bytes=VMEM_BYTES),
    )(q_nope, q_rope, w_uk)

    first_pos = block_count * block_len - query_count * owners + my_index * query_count
    limits = first_pos + jnp.arange(group_count, dtype=jnp.int32) * group_size - selection[:, 0] * block_len
    return pl.pallas_call(
        functools.partial(attention_kernel, scale, block_len),
        out_shape=out_shape,
        in_specs=[smem, smem, vmem, vmem, vmem],
        out_specs=vmem,
        scratch_shapes=[
            pltpu.VMEM((head_count * group_size, pick_count * block_len), jnp.float32),
            pltpu.VMEM((group_count, head_count * group_size, latent), jnp.bfloat16),
        ],
        compiler_params=pltpu.CompilerParams(vmem_limit_bytes=VMEM_BYTES),
    )(position[selection], limits, qfull, keys, w_uv)


def solution(mesh):
    return jax.shard_map(
        on_device,
        mesh=mesh,
        in_specs=(
            P(("groups", "ctx"), "head"),
            P(("groups", "ctx"), "head"),
            P("head", None, None),
            P("head", None, None),
            P(("groups", "ctx"), None, None),
            P(("groups", "ctx"), None),
            P("groups"),
            P(("groups", "ctx"), None),
        ),
        out_specs=P(("groups", "ctx"), "head"),
        check_vma=False,
    )
```

```python
import functools
import math

import jax
import jax.numpy as jnp
from jax import lax
from jax.experimental import pallas as pl
from jax.experimental.pallas import tpu as pltpu
from jax.sharding import PartitionSpec as P

LANES = 128
PIECES = 4
VMEM_BYTES = 56 * 1024 * 1024
MESH = pl.DeviceIdType.MESH


def slot_lists(present, owned, capacity, owners):
    member = present * owned
    ranking = jnp.cumsum(member) - 1
    local_row = lax.broadcasted_iota(jnp.int32, present.shape, 0) // owners
    slot_ids = lax.broadcasted_iota(jnp.int32, (capacity,) + present.shape, 0)
    matched = (ranking[None, :] == slot_ids) & (member[None, :] > 0)
    listing = jnp.sum(jnp.where(matched, local_row[None, :], 0), axis=1)
    return (listing, jnp.where(member > 0, ranking, 0))


def pack_blocks(latent_rows, rope_rows):
    rows, block_len, latent = latent_rows.shape
    lat = latent_rows.reshape(rows, block_len, latent // LANES, LANES)
    lat = lat.transpose(0, 2, 1, 3).reshape(rows, -1, LANES)
    return jnp.concatenate([lat, rope_rows], axis=1)


def split_rope(cache_rope, block_len):
    rows = cache_rope.shape[0]
    halves = cache_rope.reshape(rows, 2, block_len // 2, -1)
    return halves.transpose(0, 2, 1, 3).reshape(rows, block_len // 2, -1)


def project_queries(nope_ref, rope_ref, uk_ref, qfull_ref, first, end):
    head_count, head_dim, latent = uk_ref.shape
    groups = qfull_ref.shape[0]
    size = qfull_ref.shape[1] // head_count
    half = LANES // 2

    def one_pair(pair, carry):
        slab = rope_ref[:, pl.ds(pl.multiple_of(pair * LANES, LANES), LANES)].astype(jnp.float32)
        turned = pltpu.roll(slab, half, 1)
        low = lax.broadcasted_iota(jnp.int32, slab.shape, 1) < half
        twice = (jnp.where(low, slab, turned), jnp.where(low, turned, slab))
        for odd in range(2):
            head = pair * 2 + odd
            query = nope_ref[:, pl.ds(pl.multiple_of(head * head_dim, LANES), head_dim)]
            lat = jnp.dot(query, uk_ref[head], preferred_element_type=jnp.float32)
            lat = lat.astype(jnp.bfloat16).reshape(groups, size, latent)
            rot = twice[odd].astype(jnp.bfloat16).reshape(groups, size, LANES)
            at = pl.ds(pl.multiple_of(head * size, size), size)
            qfull_ref[:, at, :latent] = lat
            qfull_ref[:, at, latent:] = rot
        return carry

    lax.fori_loop(first, end, one_pair, 0)


def query_kernel(nope_ref, rope_ref, uk_ref, qfull_ref):
    project_queries(nope_ref, rope_ref, uk_ref, qfull_ref, 0, uk_ref.shape[0] // 2)


def order_lists(sel_ref, owner_ref, order_ref, owners, cache_rows, late_owner, first_pos, size, block_len):
    groups, picks = sel_ref.shape
    sel = sel_ref[...]
    lane = lax.broadcasted_iota(jnp.int32, (groups, picks), 1)

    def find(b, found):
        return jnp.where(sel == b, owner_ref[b], found)

    owner = lax.fori_loop(0, owner_ref.shape[0], find, jnp.zeros_like(sel))
    row = owner * cache_rows + sel // owners
    key = jnp.where(lane == 0, 2 * picks, jnp.where(owner == late_owner, picks, 0)) + lane
    rank = jnp.zeros_like(sel)
    for j in range(picks):
        rank = rank + (key[:, j:j + 1] < key).astype(jnp.int32)
    wide = lax.broadcasted_iota(jnp.int32, (groups, LANES), 1)
    placed = jnp.zeros((groups, LANES), jnp.int32)
    for j in range(picks):
        placed = placed + jnp.where(rank[:, j:j + 1] == wide, row[:, j:j + 1], 0)
    at = lax.broadcasted_iota(jnp.int32, (groups, LANES), 0)
    behind = first_pos + at * size - sel[:, 0:1] * block_len
    order_ref[...] = jnp.where(wide == LANES - 1, behind, placed)


def fused_kernel(
    ctx_size, head_size, capacity, scale, owner_ref, sel_ref, lat_ref, krope_ref, nope_hbm, rope_hbm, uk_hbm, uv_hbm,
    out_ref, all_ref, late_ref, nope_ref, rope_ref, uk_ref, uv_ref, qfull_ref, found_ref, scores, more_scores, partial, peaks, totals, fades,
    order_vec, order, local_sem, right_send, right_recv, left_send, left_recv, x_send, x_recv, z_core_send, z_core_recv,
    x_core_send, x_core_recv,
):
    ctx = lax.axis_index("ctx")
    head = lax.axis_index("head")
    across = (head + head_size // 2) % head_size
    sibling = head + 1 - 2 * (head % 2)
    sibling_across = (sibling + head_size // 2) % head_size
    rows, block_len, latent = lat_ref.shape
    quarter = rows // head_size
    piece = quarter // PIECES
    lane_groups = latent // LANES
    head_count, _, value_dim = uv_ref.shape
    groups, picks = sel_ref.shape
    size = qfull_ref.shape[1] // head_count
    has_left = ctx > 0
    has_right = ctx < ctx_size - 1
    last = ctx_size - 2

    barrier = pltpu.get_barrier_semaphore()
    pl.semaphore_signal(barrier, inc=1, device_id={"head": across}, device_id_type=MESH)
    pl.semaphore_signal(barrier, inc=1, device_id={"head": sibling}, device_id_type=MESH)

    @pl.when(has_left)
    def _():
        pl.semaphore_signal(barrier, inc=1, device_id={"ctx": ctx - 1}, device_id_type=MESH)

    @pl.when(has_right)
    def _():
        pl.semaphore_signal(barrier, inc=1, device_id={"ctx": ctx + 1}, device_id_type=MESH)

    loads = [
        pltpu.make_async_copy(source, target, local_sem.at[at])
        for at, (source, target) in enumerate(
            ((nope_hbm, nope_ref), (rope_hbm, rope_ref), (uk_hbm, uk_ref), (uv_hbm, uv_ref))
        )
    ]
    for load in loads:
        load.start()

    def pack_row(row, carry):
        for group in range(lane_groups):
            all_ref[ctx * rows + row, group * block_len:(group + 1) * block_len, :] = lat_ref[
                row, :, group * LANES:(group + 1) * LANES
            ]
        rope = krope_ref[row]
        all_ref[ctx * rows + row, lane_groups * block_len:, :] = jnp.concatenate(
            [rope[:block_len // 2], rope[block_len // 2:]], axis=1
        )
        return carry

    lax.fori_loop(0, rows, pack_row, 0)
    pl.semaphore_wait(barrier, 2 + has_left.astype(jnp.int32) + has_right.astype(jnp.int32))

    def place(shard, part, k, step):
        at = part * quarter + k * piece
        if step == last:
            return late_ref.at[pl.ds(at, piece)]
        return all_ref.at[pl.ds(shard * rows + at, piece)]

    def hop(source, target, send, recv, device):
        return pltpu.make_async_remote_copy(
            src_ref=source, dst_ref=target, send_sem=send, recv_sem=recv, device_id=device, device_id_type=MESH
        )

    def z_copy(side, shard, k, step):
        source = place(shard, head, k, step - 1)
        target = place(shard, head, k, step)
        at = step * PIECES + k
        if side == 0:
            return hop(source, target, right_send.at[at], right_recv.at[at], {"ctx": ctx + 1})
        return hop(source, target, left_send.at[at], left_recv.at[at], {"ctx": ctx - 1})

    def local_copy(side, shard, k, step, part, send, recv, device):
        ref = place(shard, part, k, step)
        at = step * PIECES + k
        return hop(ref, ref, send.at[side, at], recv.at[side, at], {"head": device})

    def x_copy(side, shard, k, step, part):
        return local_copy(side, shard, k, step, part, x_send, x_recv, across)

    def z_core_copy(side, shard, k, step, part):
        return local_copy(side, shard, k, step, part, z_core_send, z_core_recv, sibling)

    def x_core_copy(side, shard, k, step, part):
        return local_copy(side, shard, k, step, part, x_core_send, x_core_recv, sibling)

    def sides(step):
        return (
            (0, ctx - 1 - step, ctx - 1 - step >= 0, has_right),
            (1, ctx + 1 + step, ctx + 1 + step <= ctx_size - 1, has_left),
        )

    def start_own(k, carry):
        @pl.when(has_right)
        def _():
            z_copy(0, ctx, k, 0).start()

        @pl.when(has_left)
        def _():
            z_copy(1, ctx, k, 0).start()

        return carry

    def from_z(step, k):
        for side, shard, there, onward in sides(step):

            @pl.when(there)
            def _(side=side, shard=shard, onward=onward):
                z_copy(side, shard, k, step).wait_recv()
                if step < last:

                    @pl.when(onward)
                    def _():
                        z_copy(side, shard, k, step + 1).start()

                x_copy(side, shard, k, step, head).start()
                z_core_copy(side, shard, k, step, head).start()

    def from_x(step, k):
        for side, shard, there, onward in sides(step):

            @pl.when(there)
            def _(side=side, shard=shard):
                x_copy(side, shard, k, step, across).wait_recv()
                x_core_copy(side, shard, k, step, across).start()

    def from_core(step, k):
        for side, shard, there, onward in sides(step):

            @pl.when(there)
            def _(side=side, shard=shard):
                z_core_copy(side, shard, k, step, sibling).wait_recv()
                x_core_copy(side, shard, k, step, sibling_across).wait_recv()

    lax.fori_loop(0, PIECES, start_own, 0)
    position = owner_ref.shape[0] * block_len - groups * size * ctx_size + ctx * groups * size
    late_owner = jnp.where(has_left & has_right, -1, ctx_size - 1 - ctx)
    order_lists(sel_ref, owner_ref, order_vec, ctx_size, rows, late_owner, position, size, block_len)
    to_scalar = pltpu.make_async_copy(order_vec, order, local_sem.at[4])
    to_scalar.start()
    for load in loads[:3]:
        load.wait()
    pairs = head_count // 2
    early_events = max(1, last * PIECES)
    share = -(-pairs // early_events)

    def project(at):
        project_queries(
            nope_ref, rope_ref, uk_ref, qfull_ref,
            jnp.minimum(at * share, pairs), jnp.minimum((at + 1) * share, pairs),
        )

    if last == 0:
        project(0)

    def run_step(step, with_project):
        def event(k, carry):
            from_z(step, k)
            if with_project:
                project(step * PIECES + k)

            @pl.when(k > 0)
            def _():
                from_x(step, k - 1)

            return carry

        lax.fori_loop(0, PIECES, event, 0)

    for step in range(last):
        if step > 0:
            from_x(step - 1, PIECES - 1)
        run_step(step, True)
    if last > 0:
        from_x(last - 1, PIECES - 1)

    def settle(step):
        lax.fori_loop(0, PIECES, lambda k, carry: (from_core(step, k), carry)[1], 0)

    for step in range(last):
        settle(step)
    to_scalar.wait()

    chunk = 4
    early = (picks - min(capacity, rows) - 1) // chunk * chunk if last > 0 else 0
    factor = scale * math.log2(math.e)

    def lists(first, count, final, service):
        steps = count // chunk
        query_at = lax.broadcasted_iota(jnp.int32, (qfull_ref.shape[1], LANES), 0) % size

        def rows_of(g):
            return [order[g, first + j] for j in range(count)]

        def limit_of(g):
            return order[g, LANES - 1] + query_at if final else None

        def store_top(g, top):
            peak = jnp.max(top, axis=1, keepdims=True)
            if first > 0:
                old = peaks[g]
                peak = jnp.maximum(peak, old[:, :1])
                fades[...] = jnp.exp2((old - peak) * factor)
            peaks[g] = jnp.broadcast_to(peak, peaks.shape[1:])

        def score(g, buffer):
            block_rows = rows_of(g)
            top = None
            for c in range(steps):
                top = score_step(
                    g, block_rows, limit_of(g), c, qfull_ref, all_ref, buffer, block_len, latent, chunk, top
                )
            store_top(g, top)

        def both(g, buffer, then, then_buffer):
            block_rows = rows_of(g)
            shift = peaks[g][:, :1] * factor
            if first > 0:
                fade = fades[:, :1]
                total, value = totals[g] * fade, partial[g] * fade
            else:
                total, value = jnp.zeros(totals.shape[1:], jnp.float32), None
            then_rows = None if then is None else rows_of(then)
            top = None
            for c in range(steps):
                if then is not None:
                    top = score_step(
                        then, then_rows, limit_of(then), c, qfull_ref, all_ref, then_buffer, block_len, latent,
                        chunk, top,
                    )
                total, value = weigh_step(
                    block_rows, c, all_ref, buffer, factor, shift, block_len, latent, chunk, total, value
                )
            if final:
                found = value / jnp.sum(total, axis=1, keepdims=True)
                found_ref[g] = found.astype(jnp.bfloat16)
            else:
                totals[g] = total
                partial[g] = value
            if then is not None:
                store_top(then, top)

        def serve(k):
            from_z(last, k)

            @pl.when(k > 0)
            def _():
                from_x(last, k - 1)

        score(0, scores)

        def two_lists(pair, carry):
            both(2 * pair, scores, 2 * pair + 1, more_scores)

            @pl.when(pair < groups // 2 - 1)
            def _():
                both(2 * pair + 1, more_scores, 2 * pair + 2, scores)

            @pl.when(pair == groups // 2 - 1)
            def _():
                both(2 * pair + 1, more_scores, None, None)

            if service:

                @pl.when((pair == 1) | (pair == 3))
                def _():
                    serve(pair // 2)

            return carry

        lax.fori_loop(0, groups // 2, two_lists, 0)

    served = 0
    if early > 0:
        lists(0, early, False, True)
        served = groups // 4

    def tail_event(k, carry):
        from_z(last, k)

        @pl.when(k > 0)
        def _():
            from_x(last, k - 1)

        return carry

    lax.fori_loop(served, PIECES, tail_event, 0)
    from_x(last, PIECES - 1)
    settle(last)

    @pl.when(late_owner >= 0)
    def _():
        def move(row, carry):
            all_ref[late_owner * rows + row] = late_ref[row]
            return carry

        lax.fori_loop(0, rows, move, 0)

    lists(early, picks - early, True, False)
    loads[3].wait()

    def one_head(h, carry):
        part = found_ref[:, pl.ds(pl.multiple_of(h * size, size), size), :].reshape(groups * size, latent)
        result = jnp.dot(part, uv_ref[h], preferred_element_type=jnp.float32)
        out_ref[:, pl.ds(pl.multiple_of(h * value_dim, LANES), value_dim)] = result.astype(jnp.bfloat16)
        return carry

    lax.fori_loop(0, head_count, one_head, 0)

    def finish(k, carry):
        @pl.when(has_right)
        def _():
            z_copy(0, ctx, k, 0).wait_send()

        @pl.when(has_left)
        def _():
            z_copy(1, ctx, k, 0).wait_send()

        for step in range(ctx_size - 1):
            for side, shard, there, onward in sides(step):

                @pl.when(there)
                def _(side=side, shard=shard, onward=onward, step=step):
                    x_copy(side, shard, k, step, head).wait_send()
                    z_core_copy(side, shard, k, step, head).wait_send()
                    x_core_copy(side, shard, k, step, across).wait_send()
                    if step < last:

                        @pl.when(onward)
                        def _():
                            z_copy(side, shard, k, step + 1).wait_send()

        return carry

    lax.fori_loop(0, PIECES, finish, 0)


def score_step(g, block_rows, limit, c, qfull_ref, keys_ref, scores_ref, block_len, latent, chunk, top):
    lane_groups = latent // LANES
    half = block_len // 2
    low = lax.broadcasted_iota(jnp.int32, (half, LANES), 1) < LANES // 2
    width = chunk * block_len

    def keys_of(row):
        rope = keys_ref[row, lane_groups * block_len:, :]
        zero = jnp.zeros_like(rope)
        both = jnp.concatenate([jnp.where(low, rope, zero), jnp.where(low, zero, rope)], axis=0)
        parts = [keys_ref[row, group * block_len:(group + 1) * block_len, :] for group in range(lane_groups)]
        return jnp.concatenate(parts + [both], axis=1)

    keys = jnp.concatenate([keys_of(row) for row in block_rows[c * chunk:(c + 1) * chunk]], axis=0)
    score = lax.dot_general(
        qfull_ref[g], keys, (((1,), (1,)), ((), ())), preferred_element_type=jnp.float32
    )
    if limit is not None and (c + 1) * chunk == len(block_rows):
        end_part = score[:, width - LANES:]
        token = lax.broadcasted_iota(jnp.int32, end_part.shape, 1) - (LANES - block_len)
        end_part = jnp.where((token >= 0) & (token > limit), -jnp.inf, end_part)
        score = jnp.concatenate([score[:, :width - LANES], end_part], axis=1)
    scores_ref[:, c * width:(c + 1) * width] = score
    for at in range(width // LANES):
        piece = score[:, at * LANES:(at + 1) * LANES]
        top = piece if top is None else jnp.maximum(top, piece)
    return top


def weigh_step(block_rows, c, keys_ref, scores_ref, factor, shift, block_len, latent, chunk, total, out):
    lane_groups = latent // LANES
    width = chunk * block_len

    def values_of(row):
        parts = [keys_ref[row, group * block_len:(group + 1) * block_len, :] for group in range(lane_groups)]
        return jnp.concatenate(parts, axis=1)

    weight = jnp.exp2(scores_ref[:, c * width:(c + 1) * width] * factor - shift)
    for at in range(width // LANES):
        total = total + weight[:, at * LANES:(at + 1) * LANES]
    values = jnp.concatenate([values_of(row) for row in block_rows[c * chunk:(c + 1) * chunk]], axis=0)
    more = jnp.dot(weight.astype(jnp.bfloat16), values, preferred_element_type=jnp.float32)
    return total, more if out is None else out + more


def attend(block_rows, limit, q_ref, keys_ref, scores_ref, scale, block_len, latent, chunk):
    lane_groups = latent // LANES
    size = q_ref.shape[0]
    half = block_len // 2
    low = lax.broadcasted_iota(jnp.int32, (half, LANES), 1) < LANES // 2

    def values_of(row):
        return [
            keys_ref[row, group * block_len:(group + 1) * block_len, :] for group in range(lane_groups)
        ]

    def keys_of(row):
        rope = keys_ref[row, lane_groups * block_len:, :]
        zero = jnp.zeros_like(rope)
        both = jnp.concatenate([jnp.where(low, rope, zero), jnp.where(low, zero, rope)], axis=0)
        return values_of(row) + [both]

    def stack(rows, parts_of):
        return jnp.concatenate([jnp.concatenate(parts_of(row), axis=1) for row in rows], axis=0)

    width = chunk * block_len
    count = len(block_rows) // chunk
    query = q_ref[...]
    top = None
    for c in range(count):
        keys = stack(block_rows[c * chunk:(c + 1) * chunk], keys_of)
        score = lax.dot_general(query, keys, (((1,), (1,)), ((), ())), preferred_element_type=jnp.float32)
        if c == 0:
            head_part = score[:, :LANES]
            lane = lax.broadcasted_iota(jnp.int32, head_part.shape, 1)
            barred = (lane < block_len) & (lane > limit)
            score = jnp.concatenate([jnp.where(barred, -jnp.inf, head_part), score[:, LANES:]], axis=1)
        scores_ref[:, c * width:(c + 1) * width] = score
        for at in range(width // LANES):
            part = score[:, at * LANES:(at + 1) * LANES]
            top = part if top is None else jnp.maximum(top, part)
    factor = scale * math.log2(math.e)
    shift = jnp.max(top, axis=1, keepdims=True) * factor
    total = jnp.zeros((size, LANES), jnp.float32)
    out = jnp.zeros((size, latent), jnp.float32)
    for c in range(count):
        weight = jnp.exp2(scores_ref[:, c * width:(c + 1) * width] * factor - shift)
        for at in range(width // LANES):
            total = total + weight[:, at * LANES:(at + 1) * LANES]
        values = stack(block_rows[c * chunk:(c + 1) * chunk], values_of)
        out = out + jnp.dot(weight.astype(jnp.bfloat16), values, preferred_element_type=jnp.float32)
    return out / jnp.sum(total, axis=1, keepdims=True)


def attention_kernel(
    scale, block_len, rows_ref, limit_ref, qfull_ref, keys_ref, uv_ref, out_ref, scores, out_latent
):
    head_count, latent, value_dim = uv_ref.shape
    groups = qfull_ref.shape[0]
    size = qfull_ref.shape[1] // head_count
    picks = rows_ref.shape[1]

    def one_list(g, carry):
        block_rows = [rows_ref[g, j] for j in range(picks)]
        query_at = lax.broadcasted_iota(jnp.int32, (qfull_ref.shape[1], LANES), 0) % size
        limit = limit_ref[g] + query_at
        found = attend(
            block_rows, limit, qfull_ref.at[g], keys_ref, scores, scale, block_len, latent, 4
        )
        out_latent[g] = found.astype(jnp.bfloat16)
        return carry

    lax.fori_loop(0, groups, one_list, 0)

    def one_head(h, carry):
        part = out_latent[:, pl.ds(pl.multiple_of(h * size, size), size), :].reshape(groups * size, latent)
        result = jnp.dot(part, uv_ref[h], preferred_element_type=jnp.float32)
        out_ref[:, pl.ds(pl.multiple_of(h * value_dim, LANES), value_dim)] = result.astype(jnp.bfloat16)
        return carry

    lax.fori_loop(0, head_count, one_head, 0)


def on_device(q_nope, q_rope, w_uk, w_uv, cache_latent, cache_rope, block_owner, selection):
    owners = lax.axis_size("ctx")
    heads = lax.axis_size("head")
    my_index = lax.axis_index("ctx")
    query_count = q_nope.shape[0]
    head_count, head_dim, latent = w_uk.shape
    value_dim = w_uv.shape[2]
    cache_rows, block_len = cache_latent.shape[:2]
    rope_dim = cache_rope.shape[1] // block_len
    group_count, pick_count = selection.shape
    block_count = block_owner.shape[0]
    query_blocks = query_count // block_len
    capacity = max(3 + query_blocks // 8, (2 * pick_count + 2 * query_blocks) // owners)
    group_size = query_count // group_count
    block_ids = lax.broadcasted_iota(jnp.int32, (block_count,), 0)
    packed_rows = latent // LANES * block_len + block_len // 2
    qfull_shape = jax.ShapeDtypeStruct((group_count, head_count * group_size, latent + LANES), jnp.bfloat16)
    vmem = pl.BlockSpec(memory_space=pltpu.VMEM)
    smem = pl.BlockSpec(memory_space=pltpu.SMEM)

    out_shape = jax.ShapeDtypeStruct((query_count, head_count * value_dim), jnp.bfloat16)
    scale = (head_dim + rope_dim) ** (-0.5)

    if cache_rows <= 2 * capacity:
        events = (owners - 1) * PIECES
        width = head_count * group_size
        anywhere = pl.BlockSpec(memory_space=pl.ANY)
        return pl.pallas_call(
            functools.partial(fused_kernel, owners, heads, capacity, scale),
            out_shape=out_shape,
            in_specs=[smem, vmem, vmem, vmem] + [anywhere] * 4,
            out_specs=vmem,
            scratch_shapes=[
                pltpu.VMEM((owners * cache_rows, packed_rows, LANES), jnp.bfloat16),
                pltpu.VMEM((cache_rows, packed_rows, LANES), jnp.bfloat16),
                pltpu.VMEM(q_nope.shape, jnp.bfloat16),
                pltpu.VMEM(q_rope.shape, jnp.bfloat16),
                pltpu.VMEM(w_uk.shape, jnp.bfloat16),
                pltpu.VMEM(w_uv.shape, jnp.bfloat16),
                pltpu.VMEM(qfull_shape.shape, jnp.bfloat16),
                pltpu.VMEM((group_count, width, latent), jnp.bfloat16),
                pltpu.VMEM((width, pick_count * block_len), jnp.float32),
                pltpu.VMEM((width, pick_count * block_len), jnp.float32),
                pltpu.VMEM((group_count, width, latent), jnp.float32),
                pltpu.VMEM((group_count, width, LANES), jnp.float32),
                pltpu.VMEM((group_count, width, LANES), jnp.float32),
                pltpu.VMEM((width, LANES), jnp.float32),
                pltpu.VMEM((group_count, LANES), jnp.int32),
                pltpu.SMEM((group_count, LANES), jnp.int32),
                pltpu.SemaphoreType.DMA((5,)),
            ] + [pltpu.SemaphoreType.DMA((events,))] * 4 + [pltpu.SemaphoreType.DMA((2, events))] * 6,
            compiler_params=pltpu.CompilerParams(
                collective_id=0, has_side_effects=True, vmem_limit_bytes=VMEM_BYTES
            ),
        )(block_owner, selection, cache_latent, cache_rope.reshape(cache_rows, block_len, rope_dim), q_nope, q_rope, w_uk, w_uv)
    rope_rows = split_rope(cache_rope, block_len)
    owner_ids = lax.broadcasted_iota(jnp.int32, (owners, block_count), 0)
    owned_all = (block_owner[None, :] == owner_ids).astype(jnp.int32)
    present = jnp.zeros((block_count,), jnp.int32).at[selection.reshape(-1)].set(1)
    listings, ranking = jax.vmap(lambda owned: slot_lists(present, owned, capacity, owners))(
        owned_all
    )
    position = block_owner * capacity + jnp.sum(ranking, axis=0)
    wanted = lax.all_to_all(listings, "ctx", split_axis=0, concat_axis=0, tiled=True)
    flat_rows = wanted.reshape(-1)
    asked = pack_blocks(cache_latent[flat_rows], rope_rows[flat_rows])
    asked = asked.reshape(owners, capacity, packed_rows, LANES)
    keys = lax.all_to_all(asked, "ctx", split_axis=0, concat_axis=0, tiled=True)
    keys = keys.reshape(owners * capacity, packed_rows, LANES)
    qfull = pl.pallas_call(
        query_kernel,
        out_shape=qfull_shape,
        in_specs=[vmem] * 3,
        out_specs=vmem,
        compiler_params=pltpu.CompilerParams(vmem_limit_bytes=VMEM_BYTES),
    )(q_nope, q_rope, w_uk)

    first_pos = block_count * block_len - query_count * owners + my_index * query_count
    limits = first_pos + jnp.arange(group_count, dtype=jnp.int32) * group_size - selection[:, 0] * block_len
    return pl.pallas_call(
        functools.partial(attention_kernel, scale, block_len),
        out_shape=out_shape,
        in_specs=[smem, smem, vmem, vmem, vmem],
        out_specs=vmem,
        scratch_shapes=[
            pltpu.VMEM((head_count * group_size, pick_count * block_len), jnp.float32),
            pltpu.VMEM((group_count, head_count * group_size, latent), jnp.bfloat16),
        ],
        compiler_params=pltpu.CompilerParams(vmem_limit_bytes=VMEM_BYTES),
    )(position[selection], limits, qfull, keys, w_uv)


def solution(mesh):
    return jax.shard_map(
        on_device,
        mesh=mesh,
        in_specs=(
            P(("groups", "ctx"), "head"),
            P(("groups", "ctx"), "head"),
            P("head", None, None),
            P("head", None, None),
            P(("groups", "ctx"), None, None),
            P(("groups", "ctx"), None),
            P("groups"),
            P(("groups", "ctx"), None),
        ),
        out_specs=P(("groups", "ctx"), "head"),
        check_vma=False,
    )
```
